512 devices in a mesh: ta: 32 (over y, x), gz: 8 (over z_hi, core), gy: 2 (over z_lo).
Axes of the slice: x: 4, y: 8, z: 8 (z_hi: 4, z_lo: 2; z = z_hi * 2 + z_lo), core: 2. Of those that a mesh axis runs over, the one named last changes fastest.
Arguments:
- solution_x: bfloat16 [4, 24, 32, 32, 256], P(None, None, 'ta', 'gz', 'gy'), may hold values from -6 to 6
- solution_y: bfloat16 [4, 24, 32, 32, 256], P(None, None, 'ta', 'gz', 'gy'), may hold values from -6 to 6
- links: bfloat16 [4, 18, 32, 32, 256], P(None, None, 'ta', 'gz', 'gy'), may hold values from -3.5 to 3.5
- pole_coef: float32 [4], replicated, may hold values from 0.02 to 0.2
Outputs:
- momentum: float32 [4, 18, 32, 32, 256], P(None, None, 'ta', 'gz', 'gy')
The draws below stay inside these ranges and needn't reach their ends.
All inputs are finite; a program needn't handle non-finite values.
Results may differ from the reference program's by a relative error of at most 0.0044.
Values may be sent and summed in bfloat16 or wider, within the bound.
No kernel may reach another device: no remote copies, remote signals or barrier semaphores. Data moves between devices by JAX's collectives and lax.ppermute only.
A program may use at most 64 MiB of HBM per device.

```python
import math
import jax
import jax.numpy as jnp
import numpy as np
from jax import lax

POLES = 4
NT = 32
NZ = 32
NY = 4
NX = 64


def block_scale(stream_key, shape, pieces, low, high):
    def one(dim, parts):
        draws = jax.random.uniform(jax.random.fold_in(jax.random.fold_in(stream_key, 6), dim), (parts,), jnp.float32, low / len(pieces), high / len(pieces))
        return jnp.repeat(jnp.exp(draws), shape[dim] // parts).reshape((-1,) + (1,) * (len(shape) - dim - 1))

    level = one(*pieces[0])
    for cut in pieces[1:]:
        level = level * one(*cut)
    return level


def gaussian(stream_key, dims, scale, limit, pieces=(), kind=jnp.bfloat16):
    gain = block_scale(stream_key, dims, pieces, -0.22, 0.18) if pieces else 1.0
    entries = jax.random.normal(stream_key, dims, jnp.float32) * scale * gain
    return jnp.minimum(jnp.maximum(entries, -limit), limit).astype(kind)


def setup_inputs(seed: int = 0) -> dict:
    arg_keys = jax.random.split(jax.random.key(seed), 5)
    solution_x = gaussian(arg_keys[0], (POLES, 24, NT, NZ, NY * NX), 1.0, 6.0, ((2, 32), (3, 8), (4, 2)))
    solution_y = gaussian(arg_keys[1], (POLES, 24, NT, NZ, NY * NX), 1.0, 6.0, ((2, 32), (3, 8), (4, 2)))
    links = gaussian(arg_keys[2], (4, 18, NT, NZ, NY * NX), 3 ** -0.5, 3.5, ((2, 32), (3, 8), (4, 2)))
    pole_coef = jnp.clip(jnp.exp(jax.random.uniform(arg_keys[3], (POLES,), jnp.float32, math.log(0.02), math.log(0.2))), 0.02, 0.2)
    return dict(solution_x=solution_x, solution_y=solution_y, links=links, pole_coef=pole_coef)


CLOVER_WEIGHT = 0.5


def spin_tables():
    pauli_one = np.array([[0, 1], [1, 0]], dtype=complex)
    pauli_two = np.array([[0, -1j], [1j, 0]], dtype=complex)
    pauli_three = np.array([[1, 0], [0, -1]], dtype=complex)
    blocks = [-1j * pauli_one, -1j * pauli_two, -1j * pauli_three, np.eye(2, dtype=complex)]
    gammas = []
    for block_matrix in blocks:
        matrix = np.zeros((4, 4), dtype=complex)
        matrix[0:2, 2:4] = block_matrix
        matrix[2:4, 0:2] = block_matrix.conj().T
        gammas.append(matrix)
    sigmas = []
    for lower_dir in range(4):
        for upper_dir in range(lower_dir + 1, 4):
            sigmas.append(0.5j * (gammas[lower_dir] @ gammas[upper_dir] - gammas[upper_dir] @ gammas[lower_dir]))
    return blocks, sigmas


def plane_index(first_dir, second_dir):
    plane_order = [(0, 1), (0, 2), (0, 3), (1, 2), (1, 3), (2, 3)]
    return plane_order.index((min(first_dir, second_dir), max(first_dir, second_dir)))


def apply_spin(spin_table, spinor):
    rows_out = []
    for row_index in range(spin_table.shape[0]):
        real_total = jnp.zeros_like(spinor[:, 0, 0])
        imag_total = jnp.zeros_like(spinor[:, 0, 0])
        for col_index in range(spin_table.shape[1]):
            real_coeff = float(spin_table[row_index, col_index].real)
            imag_coeff = float(spin_table[row_index, col_index].imag)
            source_real = spinor[:, 0, col_index]
            source_imag = spinor[:, 1, col_index]
            if real_coeff != 0.0:
                real_total = real_total + real_coeff * source_real
                imag_total = imag_total + real_coeff * source_imag
            if imag_coeff != 0.0:
                real_total = real_total - imag_coeff * source_imag
                imag_total = imag_total + imag_coeff * source_real
        rows_out.append(jnp.stack([real_total, imag_total], axis=1))
    return jnp.stack(rows_out, axis=2)


def half_spinor(spinor, direction, sign_value, blocks):
    lower_part = apply_spin(sign_value * blocks[direction], spinor[:, :, 2:4])
    return (spinor[:, :, 0:2] + lower_part).astype(jnp.bfloat16)


def widened(values):
    return lax.optimization_barrier(values).astype(jnp.float32)


def outer_sum(pole_coef, left_spinor, right_spinor):
    real_total = 0.0
    imag_total = 0.0
    for pole_index in range(left_spinor.shape[0]):
        left_real = left_spinor[pole_index, 0][:, :, None]
        left_imag = left_spinor[pole_index, 1][:, :, None]
        right_real = right_spinor[pole_index, 0][:, None, :]
        right_imag = right_spinor[pole_index, 1][:, None, :]
        real_part = jnp.sum(left_real * right_real + left_imag * right_imag, axis=0)
        imag_part = jnp.sum(left_imag * right_real - left_real * right_imag, axis=0)
        real_total = real_total + pole_coef[pole_index] * real_part
        imag_total = imag_total + pole_coef[pole_index] * imag_part
    return jnp.stack([real_total, imag_total])


def color_product(left_matrix, right_matrix):
    def real_product(left_part, right_part):
        return jnp.sum(left_part[:, :, None] * right_part[None, :, :], axis=1)

    real_out = real_product(left_matrix[0], right_matrix[0]) - real_product(left_matrix[1], right_matrix[1])
    imag_out = real_product(left_matrix[0], right_matrix[1]) + real_product(left_matrix[1], right_matrix[0])
    return jnp.stack([real_out, imag_out])


def adjoint(matrix):
    swapped = jnp.swapaxes(matrix, 1, 2)
    return jnp.stack([swapped[0], -swapped[1]])


def corner_terms(corner_a, corner_b, corner_c, corner_d, link_one, link_two, link_three):
    second_factor = adjoint(link_two)
    third_factor = adjoint(link_three)
    tail_product = color_product(second_factor, third_factor)
    whole_loop = color_product(link_one, tail_product)
    middle = color_product(corner_b, tail_product) + color_product(second_factor, color_product(corner_c, third_factor))
    return color_product(corner_a, whole_loop) + color_product(whole_loop, corner_d) + color_product(link_one, middle)


def project_algebra(matrix):
    real_part = 0.5 * (matrix[0] - jnp.swapaxes(matrix[0], 0, 1))
    imag_part = 0.5 * (matrix[1] + jnp.swapaxes(matrix[1], 0, 1))
    trace_imag = (matrix[1][0, 0] + matrix[1][1, 1] + matrix[1][2, 2]) / 3.0
    identity = jnp.eye(3, dtype=matrix.dtype).reshape((3, 3) + (1,) * (matrix.ndim - 3))
    return jnp.stack([real_part, imag_part - identity * trace_imag])


def neighbour(field, direction):
    return jnp.roll(field, -1, axis=field.ndim - 1 - direction)


def reference(solution_x, solution_y, links, pole_coef):
    blocks, sigmas = spin_tables()
    site_shape = (NT, NZ, NY, NX)
    float_x = solution_x.astype(jnp.float32).reshape((POLES, 2, 4, 3) + site_shape)
    float_y = solution_y.astype(jnp.float32).reshape((POLES, 2, 4, 3) + site_shape)
    gauge_field = links.astype(jnp.float32).reshape((4, 2, 3, 3) + site_shape)
    lambdas = []
    for plane_id in range(6):
        plane_value = outer_sum(pole_coef, apply_spin(sigmas[plane_id], float_x), float_y)
        plane_value = plane_value + outer_sum(pole_coef, apply_spin(sigmas[plane_id], float_y), float_x)
        lambdas.append(widened(plane_value.astype(jnp.bfloat16)))
    outputs = []
    for link_dir in range(4):
        minus_x = widened(half_spinor(float_x, link_dir, -1.0, blocks))
        minus_y = widened(half_spinor(float_y, link_dir, -1.0, blocks))
        plus_x = widened(half_spinor(float_x, link_dir, 1.0, blocks))
        plus_y = widened(half_spinor(float_y, link_dir, 1.0, blocks))
        hop_matrix = outer_sum(pole_coef, neighbour(minus_x, link_dir), minus_y)
        hop_matrix = hop_matrix + outer_sum(pole_coef, neighbour(plus_y, link_dir), plus_x)
        staple = jnp.zeros_like(hop_matrix)
        other_dirs = [other_dir for other_dir in range(4) if other_dir != link_dir]
        for other_dir in other_dirs:
            plane_sign = 1.0 if link_dir < other_dir else -1.0
            here_value = plane_sign * lambdas[plane_index(link_dir, other_dir)]
            corner_a = neighbour(here_value, link_dir)
            corner_c = neighbour(here_value, other_dir)
            corner_b = neighbour(corner_a, other_dir)
            staple = staple + corner_terms(corner_a, corner_b, corner_c, here_value,
                                           neighbour(gauge_field[other_dir], link_dir),
                                           neighbour(gauge_field[link_dir], other_dir),
                                           gauge_field[other_dir])
        force_matrix = project_algebra(color_product(gauge_field[link_dir], hop_matrix + CLOVER_WEIGHT * staple))
        outputs.append(force_matrix.reshape((18, NT, NZ, NY * NX)))
    return jnp.stack(outputs)
```

```python
import jax
import jax.numpy as jnp
import numpy as np
from jax import lax
from jax.experimental import pallas as pl
from jax.experimental.pallas import tpu as pltpu
from jax.sharding import PartitionSpec as P

F32, BF16 = jnp.float32, jnp.bfloat16
LANES, CX = 128, 64
PLANES = [(0, 1), (0, 2), (0, 3), (1, 2), (1, 3), (2, 3)]
T_PAIR = ((0, 3), (1, 3))
Z_PAIRS = [((0, 2), (1, 2)), ((0, 1), (2, 3))]
OFF = [(0, 1), (0, 2), (1, 2)]

T_LINK, T_L, T_CORNER, T_ROWS = 384, 600, 720, 736
Y_REST, Y_HALF, Y_CORNER, Y_ROWS = 192, 168, 360, 384
TY_ROWS = 48
Z_LINK, Z_L, Z_ROWS = 96, 150, 192

G_UN1, G_UM1 = 8, 160
G_LM, G_LN, G_LMN, G_L0 = 312, 392, 472, 552
G_UM, G_UN = 624, 768
G_ROWS = 920


def spin_tables():
    one = np.array([[0, 1], [1, 0]], dtype=complex)
    two = np.array([[0, -1j], [1j, 0]], dtype=complex)
    three = np.array([[1, 0], [0, -1]], dtype=complex)
    pauli = [one, two, three]
    blocks = [-1j * one, -1j * two, -1j * three, np.eye(2, dtype=complex)]
    insert = []
    for m, n in PLANES:
        b, c = blocks[m], blocks[n]
        up = 0.5j * (b @ c.conj().T - c @ b.conj().T)
        low = 0.5j * (b.conj().T @ c - c.conj().T @ b)
        entry = []
        for block in (up, low):
            for j in range(3):
                sign = np.trace(block @ pauli[j]).real / 2
                if abs(sign) > 0.5:
                    entry.append((j, float(sign)))
        insert.append(entry)
    return blocks, insert


BLOCKS, INSERT = spin_tables()


def lane_index():
    return lax.broadcasted_iota(jnp.int32, (8, LANES), 1)


def roll64(v):
    return pltpu.roll(v, CX, 1)


def x_next(v):
    lanes = lax.broadcasted_iota(jnp.int32, v.shape, 1)
    return jnp.where(lanes % CX == CX - 1, pltpu.roll(v, CX - 1, 1), pltpu.roll(v, LANES - 1, 1))


def low_half(v):
    return lax.broadcasted_iota(jnp.int32, v.shape, 1) < CX


def pair_spinors(src, base, dst):
    for k in range(4):
        dst[pl.ds(192 * (k % 2) + k // 2, 96, stride=2), :] = src[base + 96 * k : base + 96 * k + 96, :].astype(F32)


def spin_part(ref, p, ri, spin, col):
    row = 192 * p + 8 * (ri * 12 + spin * 3 + col)
    return ref[row : row + 8, :]


def half_component(ref, p, ri, spin, col, m, sign):
    base = spin_part(ref, p, ri, spin, col)
    for b in range(2):
        coeff = sign * BLOCKS[m][spin, b]
        if coeff.real != 0:
            low = spin_part(ref, p, ri, 2 + b, col)
            base = base + low if coeff.real > 0 else base - low
        if coeff.imag != 0:
            low = spin_part(ref, p, 1 - ri, 2 + b, col)
            positive = (coeff.imag > 0) == (ri == 1)
            base = base + low if positive else base - low
    return base


def far_halves(xs, ys, m):
    for p in range(2):
        for term, (ref, sign) in enumerate(((xs, -1.0), (ys, 1.0))):
            for ri in range(2):
                for spin in range(2):
                    for col in range(3):
                        index = p * 24 + term * 12 + ri * 6 + spin * 3 + col
                        yield index, half_component(ref, p, ri, spin, col, m, sign)


def insertions(xs, ys, weights, ls, ld):
    matrices = []
    for chi in range(2):
        cross = {}
        third = {}

        def add(store, key, value):
            store[key] = value if key not in store else store[key] + value

        for p in range(2):
            w = weights[8 * p : 8 * p + 8, :]
            x = [[[spin_part(xs, p, ri, 2 * chi + s, c) for ri in range(2)] for c in range(3)] for s in range(2)]
            y = [[[spin_part(ys, p, ri, 2 * chi + s, c) * w for ri in range(2)] for c in range(3)] for s in range(2)]
            for c in range(3):
                for d in range(3):
                    for left, right in ((x, y), (y, x)):
                        a, b = left[1][c], right[0][d]
                        add(cross, (c, d, 0), a[0] * b[0] + a[1] * b[1])
                        add(cross, (c, d, 1), a[1] * b[0] - a[0] * b[1])
            for c in range(3):
                value = (x[0][c][0] * y[0][c][0] + x[0][c][1] * y[0][c][1]) - (
                    x[1][c][0] * y[1][c][0] + x[1][c][1] * y[1][c][1]
                )
                add(third, (c,), value)
            for c, d in OFF:
                for left, right in ((x, y), (y, x)):
                    for s in range(2):
                        a, b = left[s][c], right[s][d]
                        re = a[0] * b[0] + a[1] * b[1]
                        im = a[1] * b[0] - a[0] * b[1]
                        add(third, (c, d, 0), re if s == 0 else -re)
                        add(third, (c, d, 1), im if s == 0 else -im)
        first = [2.0 * cross[c, c, 0] for c in range(3)]
        second = [2.0 * cross[c, c, 1] for c in range(3)]
        last = [2.0 * third[(c,)] for c in range(3)]
        for c, d in OFF:
            first += [cross[c, d, 0] + cross[d, c, 0], cross[c, d, 1] - cross[d, c, 1]]
            second += [cross[c, d, 1] + cross[d, c, 1], cross[d, c, 0] - cross[c, d, 0]]
            last += [third[c, d, 0], third[c, d, 1]]
        matrices.append((first, second, last))
    for plane in range(6):
        (up, up_sign), (low, low_sign) = INSERT[plane]
        for e in range(9):
            a, b = matrices[0][up][e], matrices[1][low][e]
            value = a + b if up_sign * low_sign > 0 else a - b
            row = (plane * 9 + e) * 8
            ls[row : row + 8, :] = value if up_sign > 0 else -value
    ld[...] = ls[pl.ds(0, 216, stride=2), :] + ls[pl.ds(1, 216, stride=2), :]


def plane_rows(m, n):
    base = 36 * PLANES.index((min(m, n), max(m, n)))
    return slice(base, base + 36)


def first_kernel(
    all_ref, coef, xs, ys, us, ld, weights, t_out, y_out, ty_out, z_out, ls, ts, hs, ds, ys2, zs
):
    pair_spinors(all_ref, 0, xs)
    pair_spinors(all_ref, 384, ys)
    us[...] = all_ref[768:1056, :].astype(F32)
    even = lax.broadcasted_iota(jnp.int32, (8, LANES), 0) % 2 == 0
    spread = [jnp.broadcast_to(coef[0:1, k : k + 1], (8, LANES)) for k in range(4)]
    for p in range(2):
        weights[8 * p : 8 * p + 8, :] = jnp.where(even, spread[p], spread[p + 2])
    insertions(xs, ys, weights, ls, ld)
    for index, value in far_halves(xs, ys, 3):
        ts[8 * index : 8 * index + 8, :] = value
    ts[T_LINK : T_LINK + 216, :] = us[0:216, :]
    for slot, m in enumerate((0, 1, 2)):
        ts[T_L + 36 * slot : T_L + 36 * slot + 36, :] = ld[plane_rows(m, 3), :]
    ts[T_L + 108 : T_ROWS, :] = jnp.zeros((T_ROWS - T_L - 108, LANES), F32)
    ts[T_CORNER : T_CORNER + 9, :] = ld[pl.ds(plane_rows(2, 3).start, 9, stride=4), :]
    t_out[...] = ts[...].astype(BF16)
    for index, value in far_halves(xs, ys, 1):
        hs[8 * index : 8 * index + 8, :] = value
    first, second = hs[0:192, :], hs[192:384, :]
    ys2[0:192, :] = jnp.where(low_half(first), first, roll64(second))
    for slot, n in enumerate((0, 2, 3)):
        ds[72 * slot : 72 * slot + 72, :] = us[72 * n : 72 * n + 72, :]
        ds[216 + 36 * slot : 216 + 36 * slot + 36, :] = ld[plane_rows(1, n), :]
    ds[324:336, :] = jnp.zeros((12, LANES), F32)
    first, second = ds[0:Y_HALF, :], ds[Y_HALF : 2 * Y_HALF, :]
    ys2[Y_REST : Y_REST + Y_HALF, :] = jnp.where(low_half(first), first, roll64(second))
    ys2[Y_CORNER:Y_ROWS, :] = jnp.zeros((Y_ROWS - Y_CORNER, LANES), F32)
    ys2[Y_CORNER : Y_CORNER + 9, :] = roll64(ld[pl.ds(plane_rows(1, 2).start, 9, stride=4), :])
    y_out[...] = ys2[...].astype(BF16)
    ds[0:36, :] = roll64(ld[plane_rows(1, 3), :])
    ty_out[...] = ds[0:TY_ROWS, :].astype(BF16)
    for index, value in far_halves(xs, ys, 2):
        hs[8 * index : 8 * index + 8, :] = value
    zs[0:48, :] = hs[pl.ds(0, 48, stride=8), :]
    zs[48:96, :] = hs[pl.ds(1, 48, stride=8), :]
    for slot, n in enumerate((0, 1, 3)):
        zs[Z_LINK + 18 * slot : Z_LINK + 18 * slot + 18, :] = us[pl.ds(72 * n, 18, stride=4), :]
        zs[Z_L + 9 * slot : Z_L + 9 * slot + 9, :] = ld[pl.ds(plane_rows(2, n).start, 9, stride=4), :]
    zs[Z_L + 27 : Z_ROWS, :] = jnp.zeros((Z_ROWS - Z_L - 27, LANES), F32)
    z_out[...] = zs[...].astype(BF16)


def full(ref, base):
    def get(ri, c, d):
        return ref[pl.ds(base + 8 * (ri * 9 + c * 3 + d), 8), :]

    return get


def herm(ref, base):
    def get(ri, c, d):
        if c == d:
            return None if ri else ref[pl.ds(base + 8 * c, 8), :]
        low, high = min(c, d), max(c, d)
        value = ref[pl.ds(base + 8 * (3 + 2 * OFF.index((low, high)) + ri), 8), :]
        return -value if ri and c > d else value

    return get


def dagger(get):
    def other(ri, c, d):
        value = get(ri, d, c)
        return -value if ri and value is not None else value

    return other


def dot(left, right, ri, c, d):
    total = None
    for e in range(3):
        for part in range(2):
            a, b = left(part, c, e), right(ri ^ part, e, d)
            if a is None or b is None:
                continue
            term = a * b
            if ri == 0 and part == 1:
                total = -term if total is None else total - term
            else:
                total = term if total is None else total + term
    return total


def held(get):
    table = {(ri, c, d): get(ri, c, d) for ri in range(2) for c in range(3) for d in range(3)}
    return lambda ri, c, d: table[ri, c, d]


def product(left, right, extra=None):
    table = {}
    for c in range(3):
        for d in range(3):
            for ri in range(2):
                value = dot(left, right, ri, c, d)
                if extra is not None:
                    value = value + extra(ri, c, d)
                table[ri, c, d] = value
    return lambda ri, c, d: table[ri, c, d]


def keep(ref, base, get):
    for ri in range(2):
        for c in range(3):
            for d in range(3):
                ref[pl.ds(base + 8 * (ri * 9 + c * 3 + d), 8), :] = get(ri, c, d)
    return full(ref, base)


def anti(left, right):
    entries = [dot(left, right, 1, c, c) for c in range(3)]
    for c, d in OFF:
        entries.append(dot(left, right, 0, c, d) - dot(left, right, 0, d, c))
        entries.append(dot(left, right, 1, c, d) + dot(left, right, 1, d, c))
    return entries


def stage_near(xs, ys, weights, near, base, m):
    for p in range(2):
        for term, (ref, sign) in enumerate(((ys, -1.0), (xs, 1.0))):
            for ri in range(2):
                for spin in range(2):
                    for col in range(3):
                        index = p * 24 + term * 12 + ri * 6 + spin * 3 + col
                        row = base + 8 * index
                        near[row : row + 8, :] = half_component(ref, p, ri, spin, col, m, sign) * weights[8 * p : 8 * p + 8, :]


def hop_sums(far, near, far_base, near_base, hop, hop_base):
    sums = {}
    for p in range(2):
        for term in range(2):
            for spin in range(2):

                def part(ref, base, ri, col):
                    return ref[pl.ds(base + 8 * (p * 24 + term * 12 + ri * 6 + spin * 3 + col), 8), :]

                a = [[part(far, far_base, ri, c) for ri in range(2)] for c in range(3)]
                b = [[part(near, near_base, ri, c) for ri in range(2)] for c in range(3)]
                for c in range(3):
                    for d in range(3):
                        re = a[c][0] * b[d][0] + a[c][1] * b[d][1]
                        im = a[c][1] * b[d][0] - a[c][0] * b[d][1]
                        if (c, d) in sums:
                            sums[c, d] = (sums[c, d][0] + re, sums[c, d][1] + im)
                        else:
                            sums[c, d] = (re, im)
    for c in range(3):
        for d in range(3):
            for ri in range(2):
                hop[pl.ds(hop_base + 8 * (ri * 9 + c * 3 + d), 8), :] = sums[c, d][ri]


class Neighbours:
    def __init__(self, geo, us, ld, tf=None, yf=None, tyf=None, zf=None):
        self.geo, self.us, self.ld, self.tf, self.yf, self.tyf, self.zf = geo, us, ld, tf, yf, tyf, zf

    def link(self, n):
        return self.us[72 * n : 72 * n + 72, :]

    def came_y(self, row, count):
        pieces = []
        if row < Y_HALF:
            stop = min(row + count, Y_HALF)
            pieces.append(roll64(self.yf[Y_REST + row : Y_REST + stop, :]))
            count, row = count - (stop - row), stop
        if count:
            pieces.append(self.yf[Y_REST + row - Y_HALF : Y_REST + row - Y_HALF + count, :])
        return pieces[0] if len(pieces) == 1 else jnp.concatenate(pieces, axis=0)

    def y_next(self, here, came):
        return jnp.where(low_half(here), roll64(here), came)

    def put(self, base, h, value):
        self.geo[pl.ds(base + h, value.shape[0], stride=2), :] = value

    def put_z(self, base, h, value, face):
        self.geo[pl.ds(base + h - 2, value.shape[0], stride=2), :] = value
        self.geo[pl.ds(base + h + 6, face.shape[0], stride=8), :] = face

    def link_next(self, base, h, n, m):
        slot = [k for k in range(4) if k != m].index(n)
        if m == 0:
            self.put(base, h, x_next(self.link(n)))
        elif m == 1:
            self.put(base, h, self.y_next(self.link(n), self.came_y(72 * slot, 72)))
        elif m == 2:
            self.put_z(base, h, self.link(n), self.zf[Z_LINK + 18 * slot : Z_LINK + 18 * slot + 18, :])
        else:
            self.put(base, h, self.tf[72 * slot : 72 * slot + 72, :])

    def here(self, m, n):
        return self.ld[plane_rows(m, n), :]

    def from_t(self, n):
        return self.tf[216 + 36 * n : 216 + 36 * n + 36, :]

    def from_y(self, n):
        slot = (0, 2, 3).index(n)
        return self.y_next(self.here(1, n), self.came_y(216 + 36 * slot, 36))

    def z_face(self, n):
        slot = (0, 1, 3).index(n)
        return self.zf[Z_L + 9 * slot : Z_L + 9 * slot + 9, :]

    def insertion_next(self, base, h, n, m):
        if m == 0:
            self.put(base, h, x_next(self.here(m, n)))
        elif m == 1:
            self.put(base, h, self.from_y(n))
        elif m == 2:
            self.put_z(base, h, self.here(m, n), self.z_face(n))
        else:
            self.put(base, h, self.from_t(n))

    def corner(self, base, h, m, n):
        if m == 0 and n == 1:
            self.put(base, h, x_next(self.from_y(0)))
        elif m == 0 and n == 2:
            self.put_z(base, h, x_next(self.here(0, 2)), x_next(self.z_face(0)))
        elif m == 0:
            self.put(base, h, x_next(self.from_t(0)))
        elif m == 1 and n == 2:
            face = self.z_face(1)
            came = self.zf[Z_ROWS + 16 : Z_ROWS + 25, :]
            self.put_z(base, h, self.from_y(2), jnp.where(low_half(face), roll64(face), came))
        elif m == 1:
            self.put(base, h, self.y_next(self.from_t(1), self.tyf[0:36, :]))
        else:
            self.put_z(base, h, self.from_t(2), self.zf[Z_ROWS : Z_ROWS + 9, :])

    def stage(self, base, pair):
        for h in range(2):
            m, n = pair[h]
            self.put(base + G_UM, h, self.link(m))
            self.put(base + G_UN, h, self.link(n))
            self.link_next(base + G_UN1, h, n, m)
            self.link_next(base + G_UM1, h, m, n)
            self.insertion_next(base + G_LM, h, n, m)
            self.insertion_next(base + G_LN, h, m, n)
            self.corner(base + G_LMN, h, m, n)
            self.put(base + G_L0, h, self.here(m, n))


def plane_force(geo, g, work, acc, a):
    um, un = full(geo, g + G_UM), full(geo, g + G_UN)
    un1, um1 = full(geo, g + G_UN1), full(geo, g + G_UM1)
    lm, ln, lmn, l0 = (herm(geo, g + k) for k in (G_LM, G_LN, G_LMN, G_L0))
    loop = keep(work, 0, product(un1, dagger(um1)))
    inner = keep(work, 144, product(un1, lmn))
    first = product(lm, loop)
    inner = keep(work, 288, product(inner, dagger(um1), first))
    inner = keep(work, 144, product(loop, ln, inner))
    inner = keep(work, 288, product(um, inner))
    loop = keep(work, 144, product(um, loop))
    whole = keep(work, 0, product(loop, dagger(un)))
    common = anti(inner, dagger(un))
    to_m = anti(whole, l0)
    to_n = anti(l0, whole)
    for e in range(9):
        scale = 0.5 if e < 3 else 0.25
        acc[pl.ds(a + 8 * e, 8), :] = scale * (common[e] + to_m[e])
        acc[pl.ds(a + 72 + 8 * e, 8), :] = scale * (common[e] + to_n[e])


def xy_kernel(xs, ys, weights, y_ref, hop, yf, far, near):
    yf[...] = y_ref[0:Y_REST, :].astype(F32)
    for index, value in far_halves(xs, ys, 0):
        far[8 * index : 8 * index + 8, :] = x_next(value)
    stage_near(xs, ys, weights, near, 0, 0)
    low = lane_index() < CX
    for index, value in far_halves(xs, ys, 1):
        row = 384 + 8 * index
        came = yf[8 * (index % 24) : 8 * (index % 24) + 8, :]
        if index < 24:
            far[row : row + 8, :] = roll64(jnp.where(low, came, value))
        else:
            far[row : row + 8, :] = jnp.where(low, roll64(value), came)
    stage_near(xs, ys, weights, near, 384, 1)

    def one_hop(m, carry):
        base = pl.multiple_of(m * 384, 8)
        hop_sums(far, near, base, base, hop, pl.multiple_of(m * 144, 8))
        return carry

    lax.fori_loop(0, 2, one_hop, 0)


def t_kernel(xs, ys, us, ld, weights, t_ref, y_ref, ty_ref, hop, acc, tf, yf, tyf, near, geo, work):
    tf[...] = t_ref[384:T_ROWS, :].astype(F32)
    yf[...] = y_ref[...].astype(F32)
    tyf[...] = ty_ref[...].astype(F32)
    geo[920:1304, :] = t_ref[0:384, :].astype(F32)
    stage_near(xs, ys, weights, near, 0, 3)
    hop_sums(geo, near, 920, 0, hop, 0)
    Neighbours(geo, us, ld, tf, yf, tyf).stage(0, T_PAIR)
    plane_force(geo, 0, work, acc, 0)


def last_kernel(
    xs, ys, us, ld, weights, t_ref, y_ref, z_ref, hop_xy, hop_t, acc_t, out,
    tf, yf, zf, far, near, hop, geo, work, acc,
):
    tf[...] = t_ref[384:T_ROWS, :].astype(F32)
    yf[...] = y_ref[...].astype(F32)
    zf[...] = z_ref[0 : Z_ROWS + 32, :].astype(F32)
    for index, value in far_halves(xs, ys, 2):
        far[8 + 8 * index - 2 : 8 + 8 * index + 6, :] = value
    far[pl.ds(8 + 6, 48, stride=8), :] = zf[0:48, :]
    far[pl.ds(8 + 7, 48, stride=8), :] = zf[48:96, :]
    stage_near(xs, ys, weights, near, 0, 2)
    hop_sums(far, near, 8, 0, hop, 0)
    places = Neighbours(geo, us, ld, tf, yf, None, zf)
    for pair in range(2):
        places.stage(G_ROWS * pair, Z_PAIRS[pair])

    def one_pair(pair, carry):
        plane_force(geo, pl.multiple_of(pair * G_ROWS, 8), work, acc, pl.multiple_of(pair * 144, 8))
        return carry

    lax.fori_loop(0, 2, one_pair, 0)
    acc[288:432, :] = acc_t[...]

    even = lax.broadcasted_iota(jnp.int32, (8, LANES), 0) % 2 == 0
    places.put(0, 0, places.link(0))
    places.put(0, 1, places.link(1))
    places.put(144, 0, places.link(2))
    places.put(144, 1, places.link(3))
    halves = [((hop_xy, 0), (hop_xy, 144)), ((hop, 0), (hop_t, 0))]
    for pair in range(2):
        table = {}
        for ri in range(2):
            for c in range(3):
                for d in range(3):
                    row = 8 * (ri * 9 + c * 3 + d)
                    a, b = (ref[base + row : base + row + 8, :] for ref, base in halves[pair])
                    table[ri, c, d] = jnp.where(even, a + pltpu.roll(a, 7, 0), b + pltpu.roll(b, 1, 0))
        entries = anti(full(geo, 144 * pair), lambda ri, c, d: table[ri, c, d])
        for e in range(9):
            row = 432 + 72 * pair + 8 * e
            acc[row : row + 8, :] = entries[e] if e < 3 else 0.5 * entries[e]

    sources = [
        [(0, 0), (2, 0), (4, 0), (6, 0)],
        [(0, 1), (3, 0), (4, 1), (6, 1)],
        [(1, 0), (1, 1), (2, 1), (7, 0)],
        [(3, 1), (5, 0), (5, 1), (7, 1)],
    ]
    zero = jnp.zeros((4, LANES), F32)
    for m in range(4):
        values = []
        for e in range(9):
            total = None
            for slot, h in sources[m]:
                piece = acc[pl.ds(72 * slot + 8 * e + h, 4, stride=2), :]
                total = piece if total is None else total + piece
            values.append(total)
        trace = (values[0] + values[1] + values[2]) * (1.0 / 3.0)
        for c in range(3):
            for d in range(3):
                if c == d:
                    re, im = zero, values[c] - trace
                else:
                    e = 3 + 2 * OFF.index((min(c, d), max(c, d)))
                    re, im = (values[e] if c < d else -values[e]), values[e + 1]
                row = 72 * m + 4 * (3 * c + d)
                out[row : row + 4, :] = re
                out[row + 36 : row + 40, :] = im


def vmem(rows):
    return pltpu.VMEM((rows, LANES), F32)


IN_VMEM = pl.BlockSpec(memory_space=pltpu.VMEM)


def call(kernel, name, in_specs, outs, scratch, flops, out_specs=IN_VMEM):
    shapes = [jax.ShapeDtypeStruct((rows, LANES), kind) for rows, kind in outs]
    return pl.pallas_call(
        kernel,
        out_shape=shapes,
        in_specs=in_specs,
        out_specs=[out_specs] * len(shapes),
        scratch_shapes=[vmem(k) if isinstance(k, int) else k for k in scratch],
        compiler_params=pltpu.CompilerParams(vmem_limit_bytes=24 * 1024 * 1024),
        cost_estimate=pl.CostEstimate(flops=flops, bytes_accessed=1000000, transcendentals=0),
        name=name,
    )


def passed_back(block, *axes):
    sizes = [lax.axis_size(axis) for axis in axes]
    route = []
    for place in np.ndindex(*sizes):
        source = [(k + 1) % size for k, size in zip(place, sizes)]
        route.append((int(np.ravel_multi_index(source, sizes)), int(np.ravel_multi_index(place, sizes))))
    return lax.ppermute(block, axes if len(axes) > 1 else axes[0], route)


def shards(solution_x, solution_y, links, pole_coef):
    fields = jnp.concatenate(
        [solution_x.reshape(384, LANES), solution_y.reshape(384, LANES), links.reshape(288, LANES)]
    )
    xs, ys, us, local, weights, to_t, to_y, to_ty, to_z = call(
        first_kernel,
        "pack_faces",
        [IN_VMEM] * 2,
        [(384, F32), (384, F32), (288, F32), (216, F32), (16, F32), (T_ROWS, BF16), (Y_ROWS, BF16), (TY_ROWS, BF16), (Z_ROWS, BF16)],
        [432, T_ROWS, 384, 336, Y_ROWS, Z_ROWS],
        2000000,
    )(fields, pole_coef.reshape(1, 4))
    t_came = passed_back(to_t, "ta")
    y_came = passed_back(to_y, "gy")
    ty_came = passed_back(to_ty, "ta", "gy")
    z_block = jnp.concatenate(
        [to_z, t_came[T_CORNER : T_CORNER + 16], y_came[Y_CORNER : Y_CORNER + 16], ty_came[TY_ROWS - 16 :]]
    )
    z_came = passed_back(z_block, "gz")
    (hop_xy,) = call(
        xy_kernel, "hop_xy", [IN_VMEM] * 4, [(288, F32)], [Y_REST, 768, 768], 2000000
    )(xs, ys, weights, y_came)
    hop_t, acc_t = call(
        t_kernel,
        "force_t",
        [IN_VMEM] * 8,
        [(144, F32), (144, F32)],
        [T_ROWS - 384, Y_ROWS, TY_ROWS, 384, 1304, 432],
        2000000,
    )(xs, ys, us, local, weights, t_came, y_came, ty_came)
    (force,) = call(
        last_kernel,
        "force",
        [IN_VMEM] * 11,
        [(288, F32)],
        [T_ROWS - 384, Y_ROWS, Z_ROWS + 32, 400, 384, 144, 2 * G_ROWS, 432, 576],
        4000000,
        out_specs=pl.BlockSpec(),
    )(xs, ys, us, local, weights, t_came, y_came, z_came, hop_xy, hop_t, acc_t)
    return force.reshape(links.shape)


def solution(mesh):
    placed = P(None, None, "ta", "gz", "gy")
    return jax.shard_map(
        shards, mesh=mesh, in_specs=(placed, placed, placed, P()), out_specs=placed, check_vma=False
    )
```

```python
import jax
import jax.numpy as jnp
import numpy as np
from jax import lax
from jax.experimental import pallas as pl
from jax.experimental.pallas import tpu as pltpu
from jax.sharding import PartitionSpec as P

F32, BF16 = jnp.float32, jnp.bfloat16
LANES, CX = 128, 64
PLANES = [(0, 1), (0, 2), (0, 3), (1, 2), (1, 3), (2, 3)]
T_PAIR = ((0, 3), (1, 3))
Z_PAIRS = [((0, 2), (1, 2)), ((0, 1), (2, 3))]
OFF = [(0, 1), (0, 2), (1, 2)]

T_LINK, T_L, T_CORNER, T_ROWS = 384, 600, 720, 736
Y_REST, Y_HALF, Y_CORNER, Y_ROWS = 192, 168, 360, 384
TY_ROWS = 48
Z_LINK, Z_L, Z_ROWS = 96, 150, 192

G_UN1, G_UM1 = 8, 160
G_LM, G_LN, G_LMN, G_L0 = 312, 392, 472, 552
G_UM, G_UN = 624, 768
G_ROWS = 920


def spin_tables():
    one = np.array([[0, 1], [1, 0]], dtype=complex)
    two = np.array([[0, -1j], [1j, 0]], dtype=complex)
    three = np.array([[1, 0], [0, -1]], dtype=complex)
    pauli = [one, two, three]
    blocks = [-1j * one, -1j * two, -1j * three, np.eye(2, dtype=complex)]
    insert = []
    for m, n in PLANES:
        b, c = blocks[m], blocks[n]
        up = 0.5j * (b @ c.conj().T - c @ b.conj().T)
        low = 0.5j * (b.conj().T @ c - c.conj().T @ b)
        entry = []
        for block in (up, low):
            for j in range(3):
                sign = np.trace(block @ pauli[j]).real / 2
                if abs(sign) > 0.5:
                    entry.append((j, float(sign)))
        insert.append(entry)
    return blocks, insert


BLOCKS, INSERT = spin_tables()


def lane_index():
    return lax.broadcasted_iota(jnp.int32, (8, LANES), 1)


def roll64(v):
    return pltpu.roll(v, CX, 1)


def x_next(v):
    lanes = lax.broadcasted_iota(jnp.int32, v.shape, 1)
    return jnp.where(lanes % CX == CX - 1, pltpu.roll(v, CX - 1, 1), pltpu.roll(v, LANES - 1, 1))


def low_half(v):
    return lax.broadcasted_iota(jnp.int32, v.shape, 1) < CX


def pair_spinors(src, base, dst):
    for k in range(4):
        dst[pl.ds(192 * (k % 2) + k // 2, 96, stride=2), :] = src[base + 96 * k : base + 96 * k + 96, :].astype(F32)


def spin_part(ref, p, ri, spin, col):
    row = 192 * p + 8 * (ri * 12 + spin * 3 + col)
    return ref[row : row + 8, :]


def half_component(ref, p, ri, spin, col, m, sign):
    base = spin_part(ref, p, ri, spin, col)
    for b in range(2):
        coeff = sign * BLOCKS[m][spin, b]
        if coeff.real != 0:
            low = spin_part(ref, p, ri, 2 + b, col)
            base = base + low if coeff.real > 0 else base - low
        if coeff.imag != 0:
            low = spin_part(ref, p, 1 - ri, 2 + b, col)
            positive = (coeff.imag > 0) == (ri == 1)
            base = base + low if positive else base - low
    return base


def far_halves(xs, ys, m):
    for p in range(2):
        for term, (ref, sign) in enumerate(((xs, -1.0), (ys, 1.0))):
            for ri in range(2):
                for spin in range(2):
                    for col in range(3):
                        index = p * 24 + term * 12 + ri * 6 + spin * 3 + col
                        yield index, half_component(ref, p, ri, spin, col, m, sign)


def insertions(xs, ys, weights, ls, ld):
    matrices = []
    for chi in range(2):
        cross = {}
        third = {}

        def add(store, key, value):
            store[key] = value if key not in store else store[key] + value

        for p in range(2):
            w = weights[8 * p : 8 * p + 8, :]
            x = [[[spin_part(xs, p, ri, 2 * chi + s, c) for ri in range(2)] for c in range(3)] for s in range(2)]
            y = [[[spin_part(ys, p, ri, 2 * chi + s, c) * w for ri in range(2)] for c in range(3)] for s in range(2)]
            for c in range(3):
                for d in range(3):
                    for left, right in ((x, y), (y, x)):
                        a, b = left[1][c], right[0][d]
                        add(cross, (c, d, 0), a[0] * b[0] + a[1] * b[1])
                        add(cross, (c, d, 1), a[1] * b[0] - a[0] * b[1])
            for c in range(3):
                value = (x[0][c][0] * y[0][c][0] + x[0][c][1] * y[0][c][1]) - (
                    x[1][c][0] * y[1][c][0] + x[1][c][1] * y[1][c][1]
                )
                add(third, (c,), value)
            for c, d in OFF:
                for left, right in ((x, y), (y, x)):
                    for s in range(2):
                        a, b = left[s][c], right[s][d]
                        re = a[0] * b[0] + a[1] * b[1]
                        im = a[1] * b[0] - a[0] * b[1]
                        add(third, (c, d, 0), re if s == 0 else -re)
                        add(third, (c, d, 1), im if s == 0 else -im)
        first = [2.0 * cross[c, c, 0] for c in range(3)]
        second = [2.0 * cross[c, c, 1] for c in range(3)]
        last = [2.0 * third[(c,)] for c in range(3)]
        for c, d in OFF:
            first += [cross[c, d, 0] + cross[d, c, 0], cross[c, d, 1] - cross[d, c, 1]]
            second += [cross[c, d, 1] + cross[d, c, 1], cross[d, c, 0] - cross[c, d, 0]]
            last += [third[c, d, 0], third[c, d, 1]]
        matrices.append((first, second, last))
    for plane in range(6):
        (up, up_sign), (low, low_sign) = INSERT[plane]
        for e in range(9):
            a, b = matrices[0][up][e], matrices[1][low][e]
            value = a + b if up_sign * low_sign > 0 else a - b
            row = (plane * 9 + e) * 8
            ls[row : row + 8, :] = value if up_sign > 0 else -value
    ld[...] = ls[pl.ds(0, 216, stride=2), :] + ls[pl.ds(1, 216, stride=2), :]


def plane_rows(m, n):
    base = 36 * PLANES.index((min(m, n), max(m, n)))
    return slice(base, base + 36)


def first_kernel(
    x_hbm, y_hbm, u_hbm, coef_hbm, xs, ys, us, ld, weights, t_out, y_out, ty_out, z_out,
    x_ref, y_ref, u_ref, coef, ls, ts, hs, ds, ys2, zs, sems,
):
    pairs = ((coef_hbm, coef), (x_hbm, x_ref), (y_hbm, y_ref), (u_hbm, u_ref))
    copies = [pltpu.make_async_copy(source, target, sems.at[k]) for k, (source, target) in enumerate(pairs)]
    for copy in copies:
        copy.start()
    copies[1].wait()
    pair_spinors(x_ref, 0, xs)
    copies[2].wait()
    pair_spinors(y_ref, 0, ys)
    copies[0].wait()
    even = lax.broadcasted_iota(jnp.int32, (8, LANES), 0) % 2 == 0
    for p in range(2):
        weights[8 * p : 8 * p + 8, :] = jnp.where(even, coef[p], coef[p + 2])
    insertions(xs, ys, weights, ls, ld)
    copies[3].wait()
    us[...] = u_ref[...].astype(F32)
    for index, value in far_halves(xs, ys, 3):
        ts[8 * index : 8 * index + 8, :] = value
    ts[T_LINK : T_LINK + 216, :] = us[0:216, :]
    for slot, m in enumerate((0, 1, 2)):
        ts[T_L + 36 * slot : T_L + 36 * slot + 36, :] = ld[plane_rows(m, 3), :]
    ts[T_L + 108 : T_ROWS, :] = jnp.zeros((T_ROWS - T_L - 108, LANES), F32)
    ts[T_CORNER : T_CORNER + 9, :] = ld[pl.ds(plane_rows(2, 3).start, 9, stride=4), :]
    t_out[...] = ts[...].astype(BF16)
    for index, value in far_halves(xs, ys, 1):
        hs[8 * index : 8 * index + 8, :] = value
    first, second = hs[0:192, :], hs[192:384, :]
    ys2[0:192, :] = jnp.where(low_half(first), first, roll64(second))
    for slot, n in enumerate((0, 2, 3)):
        ds[72 * slot : 72 * slot + 72, :] = us[72 * n : 72 * n + 72, :]
        ds[216 + 36 * slot : 216 + 36 * slot + 36, :] = ld[plane_rows(1, n), :]
    ds[324:336, :] = jnp.zeros((12, LANES), F32)
    first, second = ds[0:Y_HALF, :], ds[Y_HALF : 2 * Y_HALF, :]
    ys2[Y_REST : Y_REST + Y_HALF, :] = jnp.where(low_half(first), first, roll64(second))
    ys2[Y_CORNER:Y_ROWS, :] = jnp.zeros((Y_ROWS - Y_CORNER, LANES), F32)
    ys2[Y_CORNER : Y_CORNER + 9, :] = roll64(ld[pl.ds(plane_rows(1, 2).start, 9, stride=4), :])
    y_out[...] = ys2[...].astype(BF16)
    ds[0:36, :] = roll64(ld[plane_rows(1, 3), :])
    ty_out[...] = ds[0:TY_ROWS, :].astype(BF16)
    for index, value in far_halves(xs, ys, 2):
        hs[8 * index : 8 * index + 8, :] = value
    zs[0:48, :] = hs[pl.ds(0, 48, stride=8), :]
    zs[48:96, :] = hs[pl.ds(1, 48, stride=8), :]
    for slot, n in enumerate((0, 1, 3)):
        zs[Z_LINK + 18 * slot : Z_LINK + 18 * slot + 18, :] = us[pl.ds(72 * n, 18, stride=4), :]
        zs[Z_L + 9 * slot : Z_L + 9 * slot + 9, :] = ld[pl.ds(plane_rows(2, n).start, 9, stride=4), :]
    zs[Z_L + 27 : Z_ROWS, :] = jnp.zeros((Z_ROWS - Z_L - 27, LANES), F32)
    z_out[...] = zs[...].astype(BF16)


def full(ref, base):
    def get(ri, c, d):
        return ref[pl.ds(base + 8 * (ri * 9 + c * 3 + d), 8), :]

    return get


def herm(ref, base):
    def get(ri, c, d):
        if c == d:
            return None if ri else ref[pl.ds(base + 8 * c, 8), :]
        low, high = min(c, d), max(c, d)
        value = ref[pl.ds(base + 8 * (3 + 2 * OFF.index((low, high)) + ri), 8), :]
        return -value if ri and c > d else value

    return get


def dagger(get):
    def other(ri, c, d):
        value = get(ri, d, c)
        return -value if ri and value is not None else value

    return other


def dot(left, right, ri, c, d):
    total = None
    for e in range(3):
        for part in range(2):
            a, b = left(part, c, e), right(ri ^ part, e, d)
            if a is None or b is None:
                continue
            term = a * b
            if ri == 0 and part == 1:
                total = -term if total is None else total - term
            else:
                total = term if total is None else total + term
    return total


def held(get):
    table = {(ri, c, d): get(ri, c, d) for ri in range(2) for c in range(3) for d in range(3)}
    return lambda ri, c, d: table[ri, c, d]


def product(left, right, extra=None):
    table = {}
    for c in range(3):
        for d in range(3):
            for ri in range(2):
                value = dot(left, right, ri, c, d)
                if extra is not None:
                    value = value + extra(ri, c, d)
                table[ri, c, d] = value
    return lambda ri, c, d: table[ri, c, d]


def keep(ref, base, get):
    for ri in range(2):
        for c in range(3):
            for d in range(3):
                ref[pl.ds(base + 8 * (ri * 9 + c * 3 + d), 8), :] = get(ri, c, d)
    return full(ref, base)


def anti(left, right):
    entries = [dot(left, right, 1, c, c) for c in range(3)]
    for c, d in OFF:
        entries.append(dot(left, right, 0, c, d) - dot(left, right, 0, d, c))
        entries.append(dot(left, right, 1, c, d) + dot(left, right, 1, d, c))
    return entries


def stage_near(xs, ys, weights, near, base, m):
    for p in range(2):
        for term, (ref, sign) in enumerate(((ys, -1.0), (xs, 1.0))):
            for ri in range(2):
                for spin in range(2):
                    for col in range(3):
                        index = p * 24 + term * 12 + ri * 6 + spin * 3 + col
                        row = base + 8 * index
                        near[row : row + 8, :] = half_component(ref, p, ri, spin, col, m, sign) * weights[8 * p : 8 * p + 8, :]


def hop_sums(far, near, far_base, near_base, hop, hop_base):
    sums = {}
    for p in range(2):
        for term in range(2):
            for spin in range(2):

                def part(ref, base, ri, col):
                    return ref[pl.ds(base + 8 * (p * 24 + term * 12 + ri * 6 + spin * 3 + col), 8), :]

                a = [[part(far, far_base, ri, c) for ri in range(2)] for c in range(3)]
                b = [[part(near, near_base, ri, c) for ri in range(2)] for c in range(3)]
                for c in range(3):
                    for d in range(3):
                        re = a[c][0] * b[d][0] + a[c][1] * b[d][1]
                        im = a[c][1] * b[d][0] - a[c][0] * b[d][1]
                        if (c, d) in sums:
                            sums[c, d] = (sums[c, d][0] + re, sums[c, d][1] + im)
                        else:
                            sums[c, d] = (re, im)
    for c in range(3):
        for d in range(3):
            for ri in range(2):
                hop[pl.ds(hop_base + 8 * (ri * 9 + c * 3 + d), 8), :] = sums[c, d][ri]


class Neighbours:
    def __init__(self, geo, us, ld, tf=None, yf=None, tyf=None, zf=None):
        self.geo, self.us, self.ld, self.tf, self.yf, self.tyf, self.zf = geo, us, ld, tf, yf, tyf, zf

    def link(self, n):
        return self.us[72 * n : 72 * n + 72, :]

    def came_y(self, row, count):
        pieces = []
        if row < Y_HALF:
            stop = min(row + count, Y_HALF)
            pieces.append(roll64(self.yf[Y_REST + row : Y_REST + stop, :]))
            count, row = count - (stop - row), stop
        if count:
            pieces.append(self.yf[Y_REST + row - Y_HALF : Y_REST + row - Y_HALF + count, :])
        return pieces[0] if len(pieces) == 1 else jnp.concatenate(pieces, axis=0)

    def y_next(self, here, came):
        return jnp.where(low_half(here), roll64(here), came)

    def put(self, base, h, value):
        self.geo[pl.ds(base + h, value.shape[0], stride=2), :] = value

    def put_z(self, base, h, value, face):
        self.geo[pl.ds(base + h - 2, value.shape[0], stride=2), :] = value
        self.geo[pl.ds(base + h + 6, face.shape[0], stride=8), :] = face

    def link_next(self, base, h, n, m):
        slot = [k for k in range(4) if k != m].index(n)
        if m == 0:
            self.put(base, h, x_next(self.link(n)))
        elif m == 1:
            self.put(base, h, self.y_next(self.link(n), self.came_y(72 * slot, 72)))
        elif m == 2:
            self.put_z(base, h, self.link(n), self.zf[Z_LINK + 18 * slot : Z_LINK + 18 * slot + 18, :])
        else:
            self.put(base, h, self.tf[72 * slot : 72 * slot + 72, :])

    def here(self, m, n):
        return self.ld[plane_rows(m, n), :]

    def from_t(self, n):
        return self.tf[216 + 36 * n : 216 + 36 * n + 36, :]

    def from_y(self, n):
        slot = (0, 2, 3).index(n)
        return self.y_next(self.here(1, n), self.came_y(216 + 36 * slot, 36))

    def z_face(self, n):
        slot = (0, 1, 3).index(n)
        return self.zf[Z_L + 9 * slot : Z_L + 9 * slot + 9, :]

    def insertion_next(self, base, h, n, m):
        if m == 0:
            self.put(base, h, x_next(self.here(m, n)))
        elif m == 1:
            self.put(base, h, self.from_y(n))
        elif m == 2:
            self.put_z(base, h, self.here(m, n), self.z_face(n))
        else:
            self.put(base, h, self.from_t(n))

    def corner(self, base, h, m, n):
        if m == 0 and n == 1:
            self.put(base, h, x_next(self.from_y(0)))
        elif m == 0 and n == 2:
            self.put_z(base, h, x_next(self.here(0, 2)), x_next(self.z_face(0)))
        elif m == 0:
            self.put(base, h, x_next(self.from_t(0)))
        elif m == 1 and n == 2:
            face = self.z_face(1)
            came = self.zf[Z_ROWS + 16 : Z_ROWS + 25, :]
            self.put_z(base, h, self.from_y(2), jnp.where(low_half(face), roll64(face), came))
        elif m == 1:
            self.put(base, h, self.y_next(self.from_t(1), self.tyf[0:36, :]))
        else:
            self.put_z(base, h, self.from_t(2), self.zf[Z_ROWS : Z_ROWS + 9, :])

    def stage(self, base, pair):
        for h in range(2):
            m, n = pair[h]
            self.put(base + G_UM, h, self.link(m))
            self.put(base + G_UN, h, self.link(n))
            self.link_next(base + G_UN1, h, n, m)
            self.link_next(base + G_UM1, h, m, n)
            self.insertion_next(base + G_LM, h, n, m)
            self.insertion_next(base + G_LN, h, m, n)
            self.corner(base + G_LMN, h, m, n)
            self.put(base + G_L0, h, self.here(m, n))


def plane_force(geo, g, work, acc, a):
    um, un = full(geo, g + G_UM), full(geo, g + G_UN)
    un1, um1 = full(geo, g + G_UN1), full(geo, g + G_UM1)
    lm, ln, lmn, l0 = (herm(geo, g + k) for k in (G_LM, G_LN, G_LMN, G_L0))
    loop = keep(work, 0, product(un1, dagger(um1)))
    inner = keep(work, 144, product(un1, lmn))
    first = product(lm, loop)
    inner = keep(work, 288, product(inner, dagger(um1), first))
    inner = keep(work, 144, product(loop, ln, inner))
    inner = keep(work, 288, product(um, inner))
    loop = keep(work, 144, product(um, loop))
    whole = keep(work, 0, product(loop, dagger(un)))
    common = anti(inner, dagger(un))
    to_m = anti(whole, l0)
    to_n = anti(l0, whole)
    for e in range(9):
        scale = 0.5 if e < 3 else 0.25
        acc[pl.ds(a + 8 * e, 8), :] = scale * (common[e] + to_m[e])
        acc[pl.ds(a + 72 + 8 * e, 8), :] = scale * (common[e] + to_n[e])


def xy_kernel(xs, ys, weights, y_ref, hop, yf, far, near):
    yf[...] = y_ref[0:Y_REST, :].astype(F32)
    for index, value in far_halves(xs, ys, 0):
        far[8 * index : 8 * index + 8, :] = x_next(value)
    stage_near(xs, ys, weights, near, 0, 0)
    low = lane_index() < CX
    for index, value in far_halves(xs, ys, 1):
        row = 384 + 8 * index
        came = yf[8 * (index % 24) : 8 * (index % 24) + 8, :]
        if index < 24:
            far[row : row + 8, :] = roll64(jnp.where(low, came, value))
        else:
            far[row : row + 8, :] = jnp.where(low, roll64(value), came)
    stage_near(xs, ys, weights, near, 384, 1)

    def one_hop(m, carry):
        base = pl.multiple_of(m * 384, 8)
        hop_sums(far, near, base, base, hop, pl.multiple_of(m * 144, 8))
        return carry

    lax.fori_loop(0, 2, one_hop, 0)


def t_kernel(xs, ys, us, ld, weights, t_ref, y_ref, ty_ref, hop, acc, tf, yf, tyf, near, geo, work):
    tf[...] = t_ref[384:T_ROWS, :].astype(F32)
    yf[...] = y_ref[...].astype(F32)
    tyf[...] = ty_ref[...].astype(F32)
    geo[920:1304, :] = t_ref[0:384, :].astype(F32)
    stage_near(xs, ys, weights, near, 0, 3)
    hop_sums(geo, near, 920, 0, hop, 0)
    Neighbours(geo, us, ld, tf, yf, tyf).stage(0, T_PAIR)
    plane_force(geo, 0, work, acc, 0)


def last_kernel(
    xs, ys, us, ld, weights, t_ref, y_ref, z_ref, hop_xy, hop_t, acc_t, out,
    tf, yf, zf, far, near, hop, geo, work, acc,
):
    tf[...] = t_ref[384:T_ROWS, :].astype(F32)
    yf[...] = y_ref[...].astype(F32)
    zf[...] = z_ref[0 : Z_ROWS + 32, :].astype(F32)
    for index, value in far_halves(xs, ys, 2):
        far[8 + 8 * index - 2 : 8 + 8 * index + 6, :] = value
    far[pl.ds(8 + 6, 48, stride=8), :] = zf[0:48, :]
    far[pl.ds(8 + 7, 48, stride=8), :] = zf[48:96, :]
    stage_near(xs, ys, weights, near, 0, 2)
    hop_sums(far, near, 8, 0, hop, 0)
    places = Neighbours(geo, us, ld, tf, yf, None, zf)
    for pair in range(2):
        places.stage(G_ROWS * pair, Z_PAIRS[pair])

    def one_pair(pair, carry):
        plane_force(geo, pl.multiple_of(pair * G_ROWS, 8), work, acc, pl.multiple_of(pair * 144, 8))
        return carry

    lax.fori_loop(0, 2, one_pair, 0)
    acc[288:432, :] = acc_t[...]

    even = lax.broadcasted_iota(jnp.int32, (8, LANES), 0) % 2 == 0
    places.put(0, 0, places.link(0))
    places.put(0, 1, places.link(1))
    places.put(144, 0, places.link(2))
    places.put(144, 1, places.link(3))
    halves = [((hop_xy, 0), (hop_xy, 144)), ((hop, 0), (hop_t, 0))]
    for pair in range(2):
        table = {}
        for ri in range(2):
            for c in range(3):
                for d in range(3):
                    row = 8 * (ri * 9 + c * 3 + d)
                    a, b = (ref[base + row : base + row + 8, :] for ref, base in halves[pair])
                    table[ri, c, d] = jnp.where(even, a + pltpu.roll(a, 7, 0), b + pltpu.roll(b, 1, 0))
        entries = anti(full(geo, 144 * pair), lambda ri, c, d: table[ri, c, d])
        for e in range(9):
            row = 432 + 72 * pair + 8 * e
            acc[row : row + 8, :] = entries[e] if e < 3 else 0.5 * entries[e]

    sources = [
        [(0, 0), (2, 0), (4, 0), (6, 0)],
        [(0, 1), (3, 0), (4, 1), (6, 1)],
        [(1, 0), (1, 1), (2, 1), (7, 0)],
        [(3, 1), (5, 0), (5, 1), (7, 1)],
    ]
    zero = jnp.zeros((4, LANES), F32)
    for m in range(4):
        values = []
        for e in range(9):
            total = None
            for slot, h in sources[m]:
                piece = acc[pl.ds(72 * slot + 8 * e + h, 4, stride=2), :]
                total = piece if total is None else total + piece
            values.append(total)
        trace = (values[0] + values[1] + values[2]) * (1.0 / 3.0)
        for c in range(3):
            for d in range(3):
                if c == d:
                    re, im = zero, values[c] - trace
                else:
                    e = 3 + 2 * OFF.index((min(c, d), max(c, d)))
                    re, im = (values[e] if c < d else -values[e]), values[e + 1]
                row = 72 * m + 4 * (3 * c + d)
                out[row : row + 4, :] = re
                out[row + 36 : row + 40, :] = im


def vmem(rows):
    return pltpu.VMEM((rows, LANES), F32)


IN_VMEM = pl.BlockSpec(memory_space=pltpu.VMEM)


def call(kernel, name, in_specs, outs, scratch, flops, out_specs=IN_VMEM):
    shapes = [jax.ShapeDtypeStruct((rows, LANES), kind) for rows, kind in outs]
    return pl.pallas_call(
        kernel,
        out_shape=shapes,
        in_specs=in_specs,
        out_specs=[out_specs] * len(shapes),
        scratch_shapes=[vmem(k) if isinstance(k, int) else k for k in scratch],
        compiler_params=pltpu.CompilerParams(vmem_limit_bytes=24 * 1024 * 1024),
        cost_estimate=pl.CostEstimate(flops=flops, bytes_accessed=1000000, transcendentals=0),
        name=name,
    )


def passed_back(block, *axes):
    sizes = [lax.axis_size(axis) for axis in axes]
    route = []
    for place in np.ndindex(*sizes):
        source = [(k + 1) % size for k, size in zip(place, sizes)]
        route.append((int(np.ravel_multi_index(source, sizes)), int(np.ravel_multi_index(place, sizes))))
    return lax.ppermute(block, axes if len(axes) > 1 else axes[0], route)


def shards(solution_x, solution_y, links, pole_coef):
    inputs = [solution_x.reshape(384, LANES), solution_y.reshape(384, LANES), links.reshape(288, LANES), pole_coef]
    xs, ys, us, local, weights, to_t, to_y, to_ty, to_z = call(
        first_kernel,
        "pack_faces",
        [pl.BlockSpec(memory_space=pltpu.HBM)] * 4,
        [(384, F32), (384, F32), (288, F32), (216, F32), (16, F32), (T_ROWS, BF16), (Y_ROWS, BF16), (TY_ROWS, BF16), (Z_ROWS, BF16)],
        [pltpu.VMEM((384, LANES), BF16)] * 2
        + [pltpu.VMEM((288, LANES), BF16), pltpu.SMEM((4,), F32), 432, T_ROWS, 384, 336, Y_ROWS, Z_ROWS, pltpu.SemaphoreType.DMA((4,))],
        2000000,
    )(*[pltpu.with_memory_space_constraint(array, pltpu.HBM) for array in inputs])
    t_came = passed_back(to_t, "ta")
    y_came = passed_back(to_y, "gy")
    ty_came = passed_back(to_ty, "ta", "gy")
    z_block = jnp.concatenate(
        [to_z, t_came[T_CORNER : T_CORNER + 16], y_came[Y_CORNER : Y_CORNER + 16], ty_came[TY_ROWS - 16 :]]
    )
    z_came = passed_back(z_block, "gz")
    (hop_xy,) = call(
        xy_kernel, "hop_xy", [IN_VMEM] * 4, [(288, F32)], [Y_REST, 768, 768], 2000000
    )(xs, ys, weights, y_came)
    hop_t, acc_t = call(
        t_kernel,
        "force_t",
        [IN_VMEM] * 8,
        [(144, F32), (144, F32)],
        [T_ROWS - 384, Y_ROWS, TY_ROWS, 384, 1304, 432],
        2000000,
    )(xs, ys, us, local, weights, t_came, y_came, ty_came)
    (force,) = call(
        last_kernel,
        "force",
        [IN_VMEM] * 11,
        [(288, F32)],
        [T_ROWS - 384, Y_ROWS, Z_ROWS + 32, 400, 384, 144, 2 * G_ROWS, 432, 576],
        4000000,
        out_specs=pl.BlockSpec(),
    )(xs, ys, us, local, weights, t_came, y_came, z_came, hop_xy, hop_t, acc_t)
    return force.reshape(links.shape)


def solution(mesh):
    placed = P(None, None, "ta", "gz", "gy")
    return jax.shard_map(
        shards, mesh=mesh, in_specs=(placed, placed, placed, P()), out_specs=placed, check_vma=False
    )
```

```python
import jax
import jax.numpy as jnp
import numpy as np
from jax import lax
from jax.experimental import pallas as pl
from jax.experimental.pallas import tpu as pltpu
from jax.sharding import PartitionSpec as P

F32, BF16 = jnp.float32, jnp.bfloat16
LANES, CX = 128, 64
PLANES = [(0, 1), (0, 2), (0, 3), (1, 2), (1, 3), (2, 3)]
T_PAIR = ((0, 3), (1, 3))
Z_PAIRS = [((0, 2), (1, 2)), ((0, 1), (2, 3))]
OFF = [(0, 1), (0, 2), (1, 2)]

L_XT, L_ZT, L_CORNER, L_ROWS = 48, 84, 128, 144
T_LINK, T_ROWS = 384, 608
Y_REST, Y_HALF, Y_CORNER, Y_ROWS = 192, 168, 360, 384
Z_LINK, Z_L, Z_ROWS = 96, 150, 192

G_UN1, G_UM1 = 8, 160
G_LM, G_LN, G_LMN, G_L0 = 312, 392, 472, 552
G_UM, G_UN = 624, 768
G_ROWS = 920


def spin_tables():
    one = np.array([[0, 1], [1, 0]], dtype=complex)
    two = np.array([[0, -1j], [1j, 0]], dtype=complex)
    three = np.array([[1, 0], [0, -1]], dtype=complex)
    pauli = [one, two, three]
    blocks = [-1j * one, -1j * two, -1j * three, np.eye(2, dtype=complex)]
    insert = []
    for m, n in PLANES:
        b, c = blocks[m], blocks[n]
        up = 0.5j * (b @ c.conj().T - c @ b.conj().T)
        low = 0.5j * (b.conj().T @ c - c.conj().T @ b)
        entry = []
        for block in (up, low):
            for j in range(3):
                sign = np.trace(block @ pauli[j]).real / 2
                if abs(sign) > 0.5:
                    entry.append((j, float(sign)))
        insert.append(entry)
    return blocks, insert


BLOCKS, INSERT = spin_tables()


def lane_index():
    return lax.broadcasted_iota(jnp.int32, (8, LANES), 1)


def roll64(v):
    return pltpu.roll(v, CX, 1)


def x_next(v):
    lanes = lax.broadcasted_iota(jnp.int32, v.shape, 1)
    return jnp.where(lanes % CX == CX - 1, pltpu.roll(v, CX - 1, 1), pltpu.roll(v, LANES - 1, 1))


def low_half(v):
    return lax.broadcasted_iota(jnp.int32, v.shape, 1) < CX


def pair_spinors(src, base, dst):
    for k in range(4):
        dst[pl.ds(192 * (k % 2) + k // 2, 96, stride=2), :] = src[base + 96 * k : base + 96 * k + 96, :].astype(F32)


def spin_part(ref, p, ri, spin, col):
    row = 192 * p + 8 * (ri * 12 + spin * 3 + col)
    return ref[row : row + 8, :]


def half_component(ref, p, ri, spin, col, m, sign):
    base = spin_part(ref, p, ri, spin, col)
    for b in range(2):
        coeff = sign * BLOCKS[m][spin, b]
        if coeff.real != 0:
            low = spin_part(ref, p, ri, 2 + b, col)
            base = base + low if coeff.real > 0 else base - low
        if coeff.imag != 0:
            low = spin_part(ref, p, 1 - ri, 2 + b, col)
            positive = (coeff.imag > 0) == (ri == 1)
            base = base + low if positive else base - low
    return base


def far_halves(xs, ys, m):
    for p in range(2):
        for term, (ref, sign) in enumerate(((xs, -1.0), (ys, 1.0))):
            for ri in range(2):
                for spin in range(2):
                    for col in range(3):
                        index = p * 24 + term * 12 + ri * 6 + spin * 3 + col
                        yield index, half_component(ref, p, ri, spin, col, m, sign)


def insertions(xs, ys, weights, ls, ld):
    matrices = []
    for chi in range(2):
        cross = {}
        third = {}

        def add(store, key, value):
            store[key] = value if key not in store else store[key] + value

        for p in range(2):
            w = weights[8 * p : 8 * p + 8, :]
            x = [[[spin_part(xs, p, ri, 2 * chi + s, c) for ri in range(2)] for c in range(3)] for s in range(2)]
            y = [[[spin_part(ys, p, ri, 2 * chi + s, c) * w for ri in range(2)] for c in range(3)] for s in range(2)]
            for c in range(3):
                for d in range(3):
                    for left, right in ((x, y), (y, x)):
                        a, b = left[1][c], right[0][d]
                        add(cross, (c, d, 0), a[0] * b[0] + a[1] * b[1])
                        add(cross, (c, d, 1), a[1] * b[0] - a[0] * b[1])
            for c in range(3):
                value = (x[0][c][0] * y[0][c][0] + x[0][c][1] * y[0][c][1]) - (
                    x[1][c][0] * y[1][c][0] + x[1][c][1] * y[1][c][1]
                )
                add(third, (c,), value)
            for c, d in OFF:
                for left, right in ((x, y), (y, x)):
                    for s in range(2):
                        a, b = left[s][c], right[s][d]
                        re = a[0] * b[0] + a[1] * b[1]
                        im = a[1] * b[0] - a[0] * b[1]
                        add(third, (c, d, 0), re if s == 0 else -re)
                        add(third, (c, d, 1), im if s == 0 else -im)
        first = [2.0 * cross[c, c, 0] for c in range(3)]
        second = [2.0 * cross[c, c, 1] for c in range(3)]
        last = [2.0 * third[(c,)] for c in range(3)]
        for c, d in OFF:
            first += [cross[c, d, 0] + cross[d, c, 0], cross[c, d, 1] - cross[d, c, 1]]
            second += [cross[c, d, 1] + cross[d, c, 1], cross[d, c, 0] - cross[c, d, 0]]
            last += [third[c, d, 0], third[c, d, 1]]
        matrices.append((first, second, last))
    for plane in range(6):
        (up, up_sign), (low, low_sign) = INSERT[plane]
        for e in range(9):
            a, b = matrices[0][up][e], matrices[1][low][e]
            value = a + b if up_sign * low_sign > 0 else a - b
            row = (plane * 9 + e) * 8
            ls[row : row + 8, :] = value if up_sign > 0 else -value
    ld[...] = ls[pl.ds(0, 216, stride=2), :] + ls[pl.ds(1, 216, stride=2), :]


def plane_rows(m, n):
    base = 36 * PLANES.index((min(m, n), max(m, n)))
    return slice(base, base + 36)


def first_kernel(
    x_hbm, y_hbm, u_hbm, coef_hbm, xs, ys, us, ld, weights, tl_out,
    x_ref, y_ref, u_ref, coef, ls, ds, sems,
):
    pairs = ((coef_hbm, coef), (x_hbm, x_ref), (y_hbm, y_ref), (u_hbm, u_ref))
    copies = [pltpu.make_async_copy(source, target, sems.at[k]) for k, (source, target) in enumerate(pairs)]
    for copy in copies:
        copy.start()
    copies[1].wait()
    pair_spinors(x_ref, 0, xs)
    copies[2].wait()
    pair_spinors(y_ref, 0, ys)
    copies[0].wait()
    even = lax.broadcasted_iota(jnp.int32, (8, LANES), 0) % 2 == 0
    for p in range(2):
        weights[8 * p : 8 * p + 8, :] = jnp.where(even, coef[p], coef[p + 2])
    insertions(xs, ys, weights, ls, ld)
    copies[3].wait()
    us[...] = u_ref[...].astype(F32)
    ds[...] = jnp.zeros((L_ROWS, LANES), F32)
    ds[0:36, :] = ld[plane_rows(1, 3), :]
    ds[L_XT : L_XT + 36, :] = ld[plane_rows(0, 3), :]
    ds[L_ZT : L_ZT + 36, :] = ld[plane_rows(2, 3), :]
    ds[L_CORNER : L_CORNER + 9, :] = ld[pl.ds(plane_rows(2, 3).start, 9, stride=4), :]
    tl_out[...] = ds[...].astype(BF16)


def y_pack_kernel(xs, ys, us, ld, y_out, hs, ds, ys2):
    for index, value in far_halves(xs, ys, 1):
        hs[8 * index : 8 * index + 8, :] = value
    first, second = hs[0:192, :], hs[192:384, :]
    ys2[0:192, :] = jnp.where(low_half(first), first, roll64(second))
    for slot, n in enumerate((0, 2, 3)):
        ds[72 * slot : 72 * slot + 72, :] = us[72 * n : 72 * n + 72, :]
        ds[216 + 36 * slot : 216 + 36 * slot + 36, :] = ld[plane_rows(1, n), :]
    ds[324:336, :] = jnp.zeros((12, LANES), F32)
    first, second = ds[0:Y_HALF, :], ds[Y_HALF : 2 * Y_HALF, :]
    ys2[Y_REST : Y_REST + Y_HALF, :] = jnp.where(low_half(first), first, roll64(second))
    ys2[Y_CORNER:Y_ROWS, :] = jnp.zeros((Y_ROWS - Y_CORNER, LANES), F32)
    ys2[Y_CORNER : Y_CORNER + 9, :] = roll64(ld[pl.ds(plane_rows(1, 2).start, 9, stride=4), :])
    y_out[...] = ys2[...].astype(BF16)


def t_pack_kernel(xs, ys, us, t_out, ts):
    for index, value in far_halves(xs, ys, 3):
        ts[8 * index : 8 * index + 8, :] = value
    ts[T_LINK : T_LINK + 216, :] = us[0:216, :]
    ts[T_LINK + 216 : T_ROWS, :] = jnp.zeros((T_ROWS - T_LINK - 216, LANES), F32)
    t_out[...] = ts[...].astype(BF16)


def z_pack_kernel(xs, ys, us, ld, tl_ref, z_out, hs, zs):
    for index, value in far_halves(xs, ys, 2):
        hs[8 * index : 8 * index + 8, :] = value
    zs[0:48, :] = hs[pl.ds(0, 48, stride=8), :]
    zs[48:96, :] = hs[pl.ds(1, 48, stride=8), :]
    for slot, n in enumerate((0, 1, 3)):
        zs[Z_LINK + 18 * slot : Z_LINK + 18 * slot + 18, :] = us[pl.ds(72 * n, 18, stride=4), :]
        zs[Z_L + 9 * slot : Z_L + 9 * slot + 9, :] = ld[pl.ds(plane_rows(2, n).start, 9, stride=4), :]
    zs[Z_L + 27 : Z_ROWS, :] = jnp.zeros((Z_ROWS - Z_L - 27, LANES), F32)
    zs[Z_ROWS : Z_ROWS + 16, :] = tl_ref[L_CORNER:L_ROWS, :].astype(F32)
    z_out[...] = zs[...].astype(BF16)


def full(ref, base):
    def get(ri, c, d):
        return ref[pl.ds(base + 8 * (ri * 9 + c * 3 + d), 8), :]

    return get


def herm(ref, base):
    def get(ri, c, d):
        if c == d:
            return None if ri else ref[pl.ds(base + 8 * c, 8), :]
        low, high = min(c, d), max(c, d)
        value = ref[pl.ds(base + 8 * (3 + 2 * OFF.index((low, high)) + ri), 8), :]
        return -value if ri and c > d else value

    return get


def dagger(get):
    def other(ri, c, d):
        value = get(ri, d, c)
        return -value if ri and value is not None else value

    return other


def dot(left, right, ri, c, d):
    total = None
    for e in range(3):
        for part in range(2):
            a, b = left(part, c, e), right(ri ^ part, e, d)
            if a is None or b is None:
                continue
            term = a * b
            if ri == 0 and part == 1:
                total = -term if total is None else total - term
            else:
                total = term if total is None else total + term
    return total


def held(get):
    table = {(ri, c, d): get(ri, c, d) for ri in range(2) for c in range(3) for d in range(3)}
    return lambda ri, c, d: table[ri, c, d]


def product(left, right, extra=None):
    table = {}
    for c in range(3):
        for d in range(3):
            for ri in range(2):
                value = dot(left, right, ri, c, d)
                if extra is not None:
                    value = value + extra(ri, c, d)
                table[ri, c, d] = value
    return lambda ri, c, d: table[ri, c, d]


def keep(ref, base, get):
    for ri in range(2):
        for c in range(3):
            for d in range(3):
                ref[pl.ds(base + 8 * (ri * 9 + c * 3 + d), 8), :] = get(ri, c, d)
    return full(ref, base)


def anti(left, right):
    entries = [dot(left, right, 1, c, c) for c in range(3)]
    for c, d in OFF:
        entries.append(dot(left, right, 0, c, d) - dot(left, right, 0, d, c))
        entries.append(dot(left, right, 1, c, d) + dot(left, right, 1, d, c))
    return entries


def stage_near(xs, ys, weights, near, base, m):
    for p in range(2):
        for term, (ref, sign) in enumerate(((ys, -1.0), (xs, 1.0))):
            for ri in range(2):
                for spin in range(2):
                    for col in range(3):
                        index = p * 24 + term * 12 + ri * 6 + spin * 3 + col
                        row = base + 8 * index
                        near[row : row + 8, :] = half_component(ref, p, ri, spin, col, m, sign) * weights[8 * p : 8 * p + 8, :]


def hop_sums(far, near, far_base, near_base, hop, hop_base):
    sums = {}
    for p in range(2):
        for term in range(2):
            for spin in range(2):

                def part(ref, base, ri, col):
                    return ref[pl.ds(base + 8 * (p * 24 + term * 12 + ri * 6 + spin * 3 + col), 8), :]

                a = [[part(far, far_base, ri, c) for ri in range(2)] for c in range(3)]
                b = [[part(near, near_base, ri, c) for ri in range(2)] for c in range(3)]
                for c in range(3):
                    for d in range(3):
                        re = a[c][0] * b[d][0] + a[c][1] * b[d][1]
                        im = a[c][1] * b[d][0] - a[c][0] * b[d][1]
                        if (c, d) in sums:
                            sums[c, d] = (sums[c, d][0] + re, sums[c, d][1] + im)
                        else:
                            sums[c, d] = (re, im)
    for c in range(3):
        for d in range(3):
            for ri in range(2):
                hop[pl.ds(hop_base + 8 * (ri * 9 + c * 3 + d), 8), :] = sums[c, d][ri]


class Neighbours:
    def __init__(self, geo, us, ld, tf=None, tl=None, yf=None, zf=None):
        self.geo, self.us, self.ld, self.tf, self.tl, self.yf, self.zf = geo, us, ld, tf, tl, yf, zf

    def link(self, n):
        return self.us[72 * n : 72 * n + 72, :]

    def came_y(self, row, count):
        pieces = []
        if row < Y_HALF:
            stop = min(row + count, Y_HALF)
            pieces.append(roll64(self.yf[Y_REST + row : Y_REST + stop, :]))
            count, row = count - (stop - row), stop
        if count:
            pieces.append(self.yf[Y_REST + row - Y_HALF : Y_REST + row - Y_HALF + count, :])
        return pieces[0] if len(pieces) == 1 else jnp.concatenate(pieces, axis=0)

    def y_next(self, here, came):
        return jnp.where(low_half(here), roll64(here), came)

    def put(self, base, h, value):
        self.geo[pl.ds(base + h, value.shape[0], stride=2), :] = value

    def put_z(self, base, h, value, face):
        self.geo[pl.ds(base + h - 2, value.shape[0], stride=2), :] = value
        self.geo[pl.ds(base + h + 6, face.shape[0], stride=8), :] = face

    def link_next(self, base, h, n, m):
        slot = [k for k in range(4) if k != m].index(n)
        if m == 0:
            self.put(base, h, x_next(self.link(n)))
        elif m == 1:
            self.put(base, h, self.y_next(self.link(n), self.came_y(72 * slot, 72)))
        elif m == 2:
            self.put_z(base, h, self.link(n), self.zf[Z_LINK + 18 * slot : Z_LINK + 18 * slot + 18, :])
        else:
            self.put(base, h, self.tf[72 * slot : 72 * slot + 72, :])

    def here(self, m, n):
        return self.ld[plane_rows(m, n), :]

    def from_t(self, n):
        row = (L_XT, 0, L_ZT)[n]
        return self.tl[row : row + 36, :]

    def from_y(self, n):
        slot = (0, 2, 3).index(n)
        return self.y_next(self.here(1, n), self.came_y(216 + 36 * slot, 36))

    def z_face(self, n):
        slot = (0, 1, 3).index(n)
        return self.zf[Z_L + 9 * slot : Z_L + 9 * slot + 9, :]

    def insertion_next(self, base, h, n, m):
        if m == 0:
            self.put(base, h, x_next(self.here(m, n)))
        elif m == 1:
            self.put(base, h, self.from_y(n))
        elif m == 2:
            self.put_z(base, h, self.here(m, n), self.z_face(n))
        else:
            self.put(base, h, self.from_t(n))

    def corner(self, base, h, m, n):
        if m == 0 and n == 1:
            self.put(base, h, x_next(self.from_y(0)))
        elif m == 0 and n == 2:
            self.put_z(base, h, x_next(self.here(0, 2)), x_next(self.z_face(0)))
        elif m == 0:
            self.put(base, h, x_next(self.from_t(0)))
        elif m == 1 and n == 2:
            face = self.z_face(1)
            came = self.zf[Z_ROWS + 16 : Z_ROWS + 25, :]
            self.put_z(base, h, self.from_y(2), jnp.where(low_half(face), roll64(face), came))
        elif m == 1:
            self.put(base, h, self.y_next(self.from_t(1), roll64(self.yf[Y_ROWS : Y_ROWS + 36, :])))
        else:
            self.put_z(base, h, self.from_t(2), self.zf[Z_ROWS : Z_ROWS + 9, :])

    def stage(self, base, pair):
        for h in range(2):
            m, n = pair[h]
            self.put(base + G_UM, h, self.link(m))
            self.put(base + G_UN, h, self.link(n))
            self.link_next(base + G_UN1, h, n, m)
            self.link_next(base + G_UM1, h, m, n)
            self.insertion_next(base + G_LM, h, n, m)
            self.insertion_next(base + G_LN, h, m, n)
            self.corner(base + G_LMN, h, m, n)
            self.put(base + G_L0, h, self.here(m, n))


def plane_force(geo, g, work, acc, a):
    um, un = full(geo, g + G_UM), full(geo, g + G_UN)
    un1, um1 = full(geo, g + G_UN1), full(geo, g + G_UM1)
    lm, ln, lmn, l0 = (herm(geo, g + k) for k in (G_LM, G_LN, G_LMN, G_L0))
    loop = keep(work, 0, product(un1, dagger(um1)))
    inner = keep(work, 144, product(un1, lmn))
    first = product(lm, loop)
    inner = keep(work, 288, product(inner, dagger(um1), first))
    inner = keep(work, 144, product(loop, ln, inner))
    inner = keep(work, 288, product(um, inner))
    loop = keep(work, 144, product(um, loop))
    whole = keep(work, 0, product(loop, dagger(un)))
    common = anti(inner, dagger(un))
    to_m = anti(whole, l0)
    to_n = anti(l0, whole)
    for e in range(9):
        scale = 0.5 if e < 3 else 0.25
        acc[pl.ds(a + 8 * e, 8), :] = scale * (common[e] + to_m[e])
        acc[pl.ds(a + 72 + 8 * e, 8), :] = scale * (common[e] + to_n[e])


def xy_kernel(xs, ys, weights, y_ref, hop, yf, far, near):
    yf[...] = y_ref[0:Y_REST, :].astype(F32)
    for index, value in far_halves(xs, ys, 0):
        far[8 * index : 8 * index + 8, :] = x_next(value)
    stage_near(xs, ys, weights, near, 0, 0)
    low = lane_index() < CX
    for index, value in far_halves(xs, ys, 1):
        row = 384 + 8 * index
        came = yf[8 * (index % 24) : 8 * (index % 24) + 8, :]
        if index < 24:
            far[row : row + 8, :] = roll64(jnp.where(low, came, value))
        else:
            far[row : row + 8, :] = jnp.where(low, roll64(value), came)
    stage_near(xs, ys, weights, near, 384, 1)

    def one_hop(m, carry):
        base = pl.multiple_of(m * 384, 8)
        hop_sums(far, near, base, base, hop, pl.multiple_of(m * 144, 8))
        return carry

    lax.fori_loop(0, 2, one_hop, 0)


def t_kernel(xs, ys, us, ld, weights, tl_ref, t_ref, y_ref, hop, acc, tl, tf, yf, near, geo, work):
    tl[...] = tl_ref[...].astype(F32)
    tf[...] = t_ref[T_LINK:T_ROWS, :].astype(F32)
    yf[...] = y_ref[...].astype(F32)
    geo[920:1304, :] = t_ref[0:384, :].astype(F32)
    stage_near(xs, ys, weights, near, 0, 3)
    hop_sums(geo, near, 920, 0, hop, 0)
    Neighbours(geo, us, ld, tf, tl, yf).stage(0, T_PAIR)
    plane_force(geo, 0, work, acc, 0)


def last_kernel(
    xs, ys, us, ld, weights, tl_ref, t_ref, y_ref, z_ref, hop_xy, hop_t, acc_t, out,
    tl, tf, yf, zf, far, near, hop, geo, work, acc,
):
    tl[...] = tl_ref[...].astype(F32)
    tf[...] = t_ref[T_LINK:T_ROWS, :].astype(F32)
    yf[...] = y_ref[...].astype(F32)
    zf[...] = z_ref[0 : Z_ROWS + 32, :].astype(F32)
    for index, value in far_halves(xs, ys, 2):
        far[8 + 8 * index - 2 : 8 + 8 * index + 6, :] = value
    far[pl.ds(8 + 6, 48, stride=8), :] = zf[0:48, :]
    far[pl.ds(8 + 7, 48, stride=8), :] = zf[48:96, :]
    stage_near(xs, ys, weights, near, 0, 2)
    hop_sums(far, near, 8, 0, hop, 0)
    places = Neighbours(geo, us, ld, tf, tl, yf, zf)
    for pair in range(2):
        places.stage(G_ROWS * pair, Z_PAIRS[pair])

    def one_pair(pair, carry):
        plane_force(geo, pl.multiple_of(pair * G_ROWS, 8), work, acc, pl.multiple_of(pair * 144, 8))
        return carry

    lax.fori_loop(0, 2, one_pair, 0)
    acc[288:432, :] = acc_t[...]

    even = lax.broadcasted_iota(jnp.int32, (8, LANES), 0) % 2 == 0
    places.put(0, 0, places.link(0))
    places.put(0, 1, places.link(1))
    places.put(144, 0, places.link(2))
    places.put(144, 1, places.link(3))
    halves = [((hop_xy, 0), (hop_xy, 144)), ((hop, 0), (hop_t, 0))]
    for pair in range(2):
        table = {}
        for ri in range(2):
            for c in range(3):
                for d in range(3):
                    row = 8 * (ri * 9 + c * 3 + d)
                    a, b = (ref[base + row : base + row + 8, :] for ref, base in halves[pair])
                    table[ri, c, d] = jnp.where(even, a + pltpu.roll(a, 7, 0), b + pltpu.roll(b, 1, 0))
        entries = anti(full(geo, 144 * pair), lambda ri, c, d: table[ri, c, d])
        for e in range(9):
            row = 432 + 72 * pair + 8 * e
            acc[row : row + 8, :] = entries[e] if e < 3 else 0.5 * entries[e]

    sources = [
        [(0, 0), (2, 0), (4, 0), (6, 0)],
        [(0, 1), (3, 0), (4, 1), (6, 1)],
        [(1, 0), (1, 1), (2, 1), (7, 0)],
        [(3, 1), (5, 0), (5, 1), (7, 1)],
    ]
    zero = jnp.zeros((4, LANES), F32)
    for m in range(4):
        values = []
        for e in range(9):
            total = None
            for slot, h in sources[m]:
                piece = acc[pl.ds(72 * slot + 8 * e + h, 4, stride=2), :]
                total = piece if total is None else total + piece
            values.append(total)
        trace = (values[0] + values[1] + values[2]) * (1.0 / 3.0)
        for c in range(3):
            for d in range(3):
                if c == d:
                    re, im = zero, values[c] - trace
                else:
                    e = 3 + 2 * OFF.index((min(c, d), max(c, d)))
                    re, im = (values[e] if c < d else -values[e]), values[e + 1]
                row = 72 * m + 4 * (3 * c + d)
                out[row : row + 4, :] = re
                out[row + 36 : row + 40, :] = im


def vmem(rows):
    return pltpu.VMEM((rows, LANES), F32)


IN_VMEM = pl.BlockSpec(memory_space=pltpu.VMEM)


def call(kernel, name, in_specs, outs, scratch, flops, out_specs=IN_VMEM):
    shapes = [jax.ShapeDtypeStruct((rows, LANES), kind) for rows, kind in outs]
    return pl.pallas_call(
        kernel,
        out_shape=shapes,
        in_specs=in_specs,
        out_specs=[out_specs] * len(shapes),
        scratch_shapes=[vmem(k) if isinstance(k, int) else k for k in scratch],
        compiler_params=pltpu.CompilerParams(vmem_limit_bytes=24 * 1024 * 1024),
        cost_estimate=pl.CostEstimate(flops=flops, bytes_accessed=1000000, transcendentals=0),
        name=name,
    )


def passed_back(block, *axes):
    sizes = [lax.axis_size(axis) for axis in axes]
    route = []
    for place in np.ndindex(*sizes):
        source = [(k + 1) % size for k, size in zip(place, sizes)]
        route.append((int(np.ravel_multi_index(source, sizes)), int(np.ravel_multi_index(place, sizes))))
    return lax.ppermute(block, axes if len(axes) > 1 else axes[0], route)


def shards(solution_x, solution_y, links, pole_coef):
    inputs = [solution_x.reshape(384, LANES), solution_y.reshape(384, LANES), links.reshape(288, LANES), pole_coef]
    xs, ys, us, local, weights, to_tl = call(
        first_kernel,
        "insertions",
        [pl.BlockSpec(memory_space=pltpu.HBM)] * 4,
        [(384, F32), (384, F32), (288, F32), (216, F32), (16, F32), (L_ROWS, BF16)],
        [pltpu.VMEM((384, LANES), BF16)] * 2
        + [pltpu.VMEM((288, LANES), BF16), pltpu.SMEM((4,), F32), 432, L_ROWS, pltpu.SemaphoreType.DMA((4,))],
        1000000,
    )(*[pltpu.with_memory_space_constraint(array, pltpu.HBM) for array in inputs])
    tl_came = passed_back(to_tl, "ta")
    (to_t,) = call(t_pack_kernel, "pack_t", [IN_VMEM] * 3, [(T_ROWS, BF16)], [T_ROWS], 500000)(xs, ys, us)
    t_came = passed_back(to_t, "ta")
    (to_y,) = call(y_pack_kernel, "pack_y", [IN_VMEM] * 4, [(Y_ROWS, BF16)], [384, 336, Y_ROWS], 500000)(xs, ys, us, local)
    y_came = passed_back(jnp.concatenate([to_y, tl_came[0:48]]), "gy")
    (to_z,) = call(z_pack_kernel, "pack_z", [IN_VMEM] * 5, [(Z_ROWS + 16, BF16)], [384, Z_ROWS + 16], 500000)(
        xs, ys, us, local, tl_came
    )
    z_block = jnp.concatenate(
        [to_z, y_came[Y_CORNER : Y_CORNER + 16], t_came[T_ROWS - 16 :]]
    )
    z_came = passed_back(z_block, "gz")
    (hop_xy,) = call(
        xy_kernel, "hop_xy", [IN_VMEM] * 4, [(288, F32)], [Y_REST, 768, 768], 2000000
    )(xs, ys, weights, y_came)
    hop_t, acc_t = call(
        t_kernel,
        "force_t",
        [IN_VMEM] * 8,
        [(144, F32), (144, F32)],
        [L_ROWS, T_ROWS - T_LINK, Y_ROWS + 48, 384, 1304, 432],
        2000000,
    )(xs, ys, us, local, weights, tl_came, t_came, y_came)
    (force,) = call(
        last_kernel,
        "force",
        [IN_VMEM] * 12,
        [(288, F32)],
        [L_ROWS, T_ROWS - T_LINK, Y_ROWS + 48, Z_ROWS + 32, 400, 384, 144, 2 * G_ROWS, 432, 576],
        4000000,
        out_specs=pl.BlockSpec(),
    )(xs, ys, us, local, weights, tl_came, t_came, y_came, z_came, hop_xy, hop_t, acc_t)
    return force.reshape(links.shape)


def solution(mesh):
    placed = P(None, None, "ta", "gz", "gy")
    return jax.shard_map(
        shards, mesh=mesh, in_specs=(placed, placed, placed, P()), out_specs=placed, check_vma=False
    )
```

```python
import jax
import jax.numpy as jnp
import numpy as np
from jax import lax
from jax.experimental import pallas as pl
from jax.experimental.pallas import tpu as pltpu
from jax.sharding import PartitionSpec as P

F32, BF16 = jnp.float32, jnp.bfloat16
LANES, CX = 128, 64
PLANES = [(0, 1), (0, 2), (0, 3), (1, 2), (1, 3), (2, 3)]
T_PAIR = ((0, 3), (1, 3))
Z_PAIRS = [((0, 2), (1, 2)), ((0, 1), (2, 3))]
OFF = [(0, 1), (0, 2), (1, 2)]

U_ROWS, LD_ROWS = 320, 256

L_XT, L_ZT, L_CORNER, L_ROWS = 48, 84, 128, 144
T_LINK, T_ROWS = 384, 608
Y_REST, Y_HALF, Y_CORNER, Y_ROWS = 192, 168, 360, 384
Z_LINK, Z_L, Z_ROWS = 96, 150, 192

G_UN1, G_UM1 = 8, 160
G_LM, G_LN, G_LMN, G_L0 = 312, 392, 472, 552
G_UM, G_UN = 624, 768
G_ROWS = 920


def spin_tables():
    one = np.array([[0, 1], [1, 0]], dtype=complex)
    two = np.array([[0, -1j], [1j, 0]], dtype=complex)
    three = np.array([[1, 0], [0, -1]], dtype=complex)
    pauli = [one, two, three]
    blocks = [-1j * one, -1j * two, -1j * three, np.eye(2, dtype=complex)]
    insert = []
    for m, n in PLANES:
        b, c = blocks[m], blocks[n]
        up = 0.5j * (b @ c.conj().T - c @ b.conj().T)
        low = 0.5j * (b.conj().T @ c - c.conj().T @ b)
        entry = []
        for block in (up, low):
            for j in range(3):
                sign = np.trace(block @ pauli[j]).real / 2
                if abs(sign) > 0.5:
                    entry.append((j, float(sign)))
        insert.append(entry)
    return blocks, insert


BLOCKS, INSERT = spin_tables()


def lane_index():
    return lax.broadcasted_iota(jnp.int32, (8, LANES), 1)


def roll64(v):
    return pltpu.roll(v, CX, 1)


def x_next(v):
    lanes = lax.broadcasted_iota(jnp.int32, v.shape, 1)
    return jnp.where(lanes % CX == CX - 1, pltpu.roll(v, CX - 1, 1), pltpu.roll(v, LANES - 1, 1))


def low_half(v):
    return lax.broadcasted_iota(jnp.int32, v.shape, 1) < CX


def pair_spinors(src, base, dst):
    for k in range(4):
        dst[pl.ds(192 * (k % 2) + k // 2, 96, stride=2), :] = src[base + 96 * k : base + 96 * k + 96, :].astype(F32)


def spin_part(ref, p, ri, spin, col):
    row = 192 * p + 8 * (ri * 12 + spin * 3 + col)
    return ref[row : row + 8, :]


def half_component(ref, p, ri, spin, col, m, sign):
    base = spin_part(ref, p, ri, spin, col)
    for b in range(2):
        coeff = sign * BLOCKS[m][spin, b]
        if coeff.real != 0:
            low = spin_part(ref, p, ri, 2 + b, col)
            base = base + low if coeff.real > 0 else base - low
        if coeff.imag != 0:
            low = spin_part(ref, p, 1 - ri, 2 + b, col)
            positive = (coeff.imag > 0) == (ri == 1)
            base = base + low if positive else base - low
    return base


def far_halves(xs, ys, m):
    for p in range(2):
        for term, (ref, sign) in enumerate(((xs, -1.0), (ys, 1.0))):
            for ri in range(2):
                for spin in range(2):
                    for col in range(3):
                        index = p * 24 + term * 12 + ri * 6 + spin * 3 + col
                        yield index, half_component(ref, p, ri, spin, col, m, sign)


def insertions(xs, ys, weights, ls, ld):
    matrices = []
    for chi in range(2):
        cross = {}
        third = {}

        def add(store, key, value):
            store[key] = value if key not in store else store[key] + value

        for p in range(2):
            w = weights[8 * p : 8 * p + 8, :]
            x = [[[spin_part(xs, p, ri, 2 * chi + s, c) for ri in range(2)] for c in range(3)] for s in range(2)]
            y = [[[spin_part(ys, p, ri, 2 * chi + s, c) * w for ri in range(2)] for c in range(3)] for s in range(2)]
            for c in range(3):
                for d in range(3):
                    for left, right in ((x, y), (y, x)):
                        a, b = left[1][c], right[0][d]
                        add(cross, (c, d, 0), a[0] * b[0] + a[1] * b[1])
                        add(cross, (c, d, 1), a[1] * b[0] - a[0] * b[1])
            for c in range(3):
                value = (x[0][c][0] * y[0][c][0] + x[0][c][1] * y[0][c][1]) - (
                    x[1][c][0] * y[1][c][0] + x[1][c][1] * y[1][c][1]
                )
                add(third, (c,), value)
            for c, d in OFF:
                for left, right in ((x, y), (y, x)):
                    for s in range(2):
                        a, b = left[s][c], right[s][d]
                        re = a[0] * b[0] + a[1] * b[1]
                        im = a[1] * b[0] - a[0] * b[1]
                        add(third, (c, d, 0), re if s == 0 else -re)
                        add(third, (c, d, 1), im if s == 0 else -im)
        first = [2.0 * cross[c, c, 0] for c in range(3)]
        second = [2.0 * cross[c, c, 1] for c in range(3)]
        last = [2.0 * third[(c,)] for c in range(3)]
        for c, d in OFF:
            first += [cross[c, d, 0] + cross[d, c, 0], cross[c, d, 1] - cross[d, c, 1]]
            second += [cross[c, d, 1] + cross[d, c, 1], cross[d, c, 0] - cross[c, d, 0]]
            last += [third[c, d, 0], third[c, d, 1]]
        matrices.append((first, second, last))
    for plane in range(6):
        (up, up_sign), (low, low_sign) = INSERT[plane]
        for e in range(9):
            a, b = matrices[0][up][e], matrices[1][low][e]
            value = a + b if up_sign * low_sign > 0 else a - b
            row = (plane * 9 + e) * 8
            ls[row : row + 8, :] = value if up_sign > 0 else -value
    ld[0:216, :] = ls[pl.ds(0, 216, stride=2), :] + ls[pl.ds(1, 216, stride=2), :]


def plane_rows(m, n):
    base = 36 * PLANES.index((min(m, n), max(m, n)))
    return slice(base, base + 36)


def first_kernel(
    x_hbm, y_hbm, u_hbm, coef_hbm, xs, ys, us, ld, weights, tl_out,
    x_ref, y_ref, u_ref, coef, ls, ds, sems,
):
    pairs = ((coef_hbm, coef), (x_hbm, x_ref), (y_hbm, y_ref), (u_hbm, u_ref))
    copies = [pltpu.make_async_copy(source, target, sems.at[k]) for k, (source, target) in enumerate(pairs)]
    for copy in copies:
        copy.start()
    copies[1].wait()
    pair_spinors(x_ref, 0, xs)
    copies[2].wait()
    pair_spinors(y_ref, 0, ys)
    copies[0].wait()
    even = lax.broadcasted_iota(jnp.int32, (8, LANES), 0) % 2 == 0
    for p in range(2):
        weights[8 * p : 8 * p + 8, :] = jnp.where(even, coef[p], coef[p + 2])
    insertions(xs, ys, weights, ls, ld)
    copies[3].wait()
    us[0:288, :] = u_ref[...].astype(F32)
    ds[...] = jnp.zeros((L_ROWS, LANES), F32)
    ds[0:36, :] = ld[plane_rows(1, 3), :]
    ds[L_XT : L_XT + 36, :] = ld[plane_rows(0, 3), :]
    ds[L_ZT : L_ZT + 36, :] = ld[plane_rows(2, 3), :]
    ds[L_CORNER : L_CORNER + 9, :] = ld[pl.ds(plane_rows(2, 3).start, 9, stride=4), :]
    tl_out[...] = ds[...].astype(BF16)


def y_pack_kernel(xs, ys, us, ld, y_out, hs, ds, ys2):
    for index, value in far_halves(xs, ys, 1):
        hs[8 * index : 8 * index + 8, :] = value
    first, second = hs[0:192, :], hs[192:384, :]
    ys2[0:192, :] = jnp.where(low_half(first), first, roll64(second))
    for slot, n in enumerate((0, 2, 3)):
        ds[72 * slot : 72 * slot + 72, :] = us[72 * n : 72 * n + 72, :]
        ds[216 + 36 * slot : 216 + 36 * slot + 36, :] = ld[plane_rows(1, n), :]
    ds[324:336, :] = jnp.zeros((12, LANES), F32)
    first, second = ds[0:Y_HALF, :], ds[Y_HALF : 2 * Y_HALF, :]
    ys2[Y_REST : Y_REST + Y_HALF, :] = jnp.where(low_half(first), first, roll64(second))
    ys2[Y_CORNER:Y_ROWS, :] = jnp.zeros((Y_ROWS - Y_CORNER, LANES), F32)
    ys2[Y_CORNER : Y_CORNER + 9, :] = roll64(ld[pl.ds(plane_rows(1, 2).start, 9, stride=4), :])
    y_out[...] = ys2[...].astype(BF16)


def t_pack_kernel(xs, ys, us, t_out, ts):
    for index, value in far_halves(xs, ys, 3):
        ts[8 * index : 8 * index + 8, :] = value
    ts[T_LINK : T_LINK + 216, :] = us[0:216, :]
    ts[T_LINK + 216 : T_ROWS, :] = jnp.zeros((T_ROWS - T_LINK - 216, LANES), F32)
    t_out[...] = ts[...].astype(BF16)


def z_pack_kernel(xs, ys, us, ld, tl_ref, z_out, hs, zs):
    for index, value in far_halves(xs, ys, 2):
        hs[8 * index : 8 * index + 8, :] = value
    zs[0:48, :] = hs[pl.ds(0, 48, stride=8), :]
    zs[48:96, :] = hs[pl.ds(1, 48, stride=8), :]
    for slot, n in enumerate((0, 1, 3)):
        zs[Z_LINK + 18 * slot : Z_LINK + 18 * slot + 18, :] = us[pl.ds(72 * n, 18, stride=4), :]
        zs[Z_L + 9 * slot : Z_L + 9 * slot + 9, :] = ld[pl.ds(plane_rows(2, n).start, 9, stride=4), :]
    zs[Z_L + 27 : Z_ROWS, :] = jnp.zeros((Z_ROWS - Z_L - 27, LANES), F32)
    zs[Z_ROWS : Z_ROWS + 16, :] = tl_ref[L_CORNER:L_ROWS, :].astype(F32)
    z_out[...] = zs[...].astype(BF16)


def full(ref, base):
    def get(ri, c, d):
        return ref[pl.ds(base + 8 * (ri * 9 + c * 3 + d), 8), :]

    return get


def herm(ref, base):
    def get(ri, c, d):
        if c == d:
            return None if ri else ref[pl.ds(base + 8 * c, 8), :]
        low, high = min(c, d), max(c, d)
        value = ref[pl.ds(base + 8 * (3 + 2 * OFF.index((low, high)) + ri), 8), :]
        return -value if ri and c > d else value

    return get


def dagger(get):
    def other(ri, c, d):
        value = get(ri, d, c)
        return -value if ri and value is not None else value

    return other


def dot(left, right, ri, c, d):
    total = None
    for e in range(3):
        for part in range(2):
            a, b = left(part, c, e), right(ri ^ part, e, d)
            if a is None or b is None:
                continue
            term = a * b
            if ri == 0 and part == 1:
                total = -term if total is None else total - term
            else:
                total = term if total is None else total + term
    return total


def held(get):
    table = {(ri, c, d): get(ri, c, d) for ri in range(2) for c in range(3) for d in range(3)}
    return lambda ri, c, d: table[ri, c, d]


def product(left, right, extra=None):
    table = {}
    for c in range(3):
        for d in range(3):
            for ri in range(2):
                value = dot(left, right, ri, c, d)
                if extra is not None:
                    value = value + extra(ri, c, d)
                table[ri, c, d] = value
    return lambda ri, c, d: table[ri, c, d]


def keep(ref, base, get):
    for ri in range(2):
        for c in range(3):
            for d in range(3):
                ref[pl.ds(base + 8 * (ri * 9 + c * 3 + d), 8), :] = get(ri, c, d)
    return full(ref, base)


def anti(left, right):
    entries = [dot(left, right, 1, c, c) for c in range(3)]
    for c, d in OFF:
        entries.append(dot(left, right, 0, c, d) - dot(left, right, 0, d, c))
        entries.append(dot(left, right, 1, c, d) + dot(left, right, 1, d, c))
    return entries


def stage_near(xs, ys, weights, near, base, m):
    for p in range(2):
        for term, (ref, sign) in enumerate(((ys, -1.0), (xs, 1.0))):
            for ri in range(2):
                for spin in range(2):
                    for col in range(3):
                        index = p * 24 + term * 12 + ri * 6 + spin * 3 + col
                        row = base + 8 * index
                        near[row : row + 8, :] = half_component(ref, p, ri, spin, col, m, sign) * weights[8 * p : 8 * p + 8, :]


def hop_sums(far, near, far_base, near_base, hop, hop_base):
    sums = {}
    for p in range(2):
        for term in range(2):
            for spin in range(2):

                def part(ref, base, ri, col):
                    return ref[pl.ds(base + 8 * (p * 24 + term * 12 + ri * 6 + spin * 3 + col), 8), :]

                a = [[part(far, far_base, ri, c) for ri in range(2)] for c in range(3)]
                b = [[part(near, near_base, ri, c) for ri in range(2)] for c in range(3)]
                for c in range(3):
                    for d in range(3):
                        re = a[c][0] * b[d][0] + a[c][1] * b[d][1]
                        im = a[c][1] * b[d][0] - a[c][0] * b[d][1]
                        if (c, d) in sums:
                            sums[c, d] = (sums[c, d][0] + re, sums[c, d][1] + im)
                        else:
                            sums[c, d] = (re, im)
    for c in range(3):
        for d in range(3):
            for ri in range(2):
                hop[pl.ds(hop_base + 8 * (ri * 9 + c * 3 + d), 8), :] = sums[c, d][ri]


class Neighbours:
    def __init__(self, geo, us, ld, tf=None, tl=None, yf=None, zf=None):
        self.geo, self.us, self.ld, self.tf, self.tl, self.yf, self.zf = geo, us, ld, tf, tl, yf, zf

    def link(self, n):
        return self.us[72 * n : 72 * n + 72, :]

    def came_y(self, row, count):
        pieces = []
        if row < Y_HALF:
            stop = min(row + count, Y_HALF)
            pieces.append(roll64(self.yf[Y_REST + row : Y_REST + stop, :]))
            count, row = count - (stop - row), stop
        if count:
            pieces.append(self.yf[Y_REST + row - Y_HALF : Y_REST + row - Y_HALF + count, :])
        return pieces[0] if len(pieces) == 1 else jnp.concatenate(pieces, axis=0)

    def y_next(self, here, came):
        return jnp.where(low_half(here), roll64(here), came)

    def put(self, base, h, value):
        self.geo[pl.ds(base + h, value.shape[0], stride=2), :] = value

    def put_z(self, base, h, value, face):
        self.geo[pl.ds(base + h - 2, value.shape[0], stride=2), :] = value
        self.geo[pl.ds(base + h + 6, face.shape[0], stride=8), :] = face

    def link_next(self, base, h, n, m):
        slot = [k for k in range(4) if k != m].index(n)
        if m == 0:
            self.put(base, h, x_next(self.link(n)))
        elif m == 1:
            self.put(base, h, self.y_next(self.link(n), self.came_y(72 * slot, 72)))
        elif m == 2:
            self.put_z(base, h, self.link(n), self.zf[Z_LINK + 18 * slot : Z_LINK + 18 * slot + 18, :])
        else:
            self.put(base, h, self.tf[72 * slot : 72 * slot + 72, :])

    def here(self, m, n):
        return self.ld[plane_rows(m, n), :]

    def from_t(self, n):
        row = (L_XT, 0, L_ZT)[n]
        return self.tl[row : row + 36, :]

    def from_y(self, n):
        slot = (0, 2, 3).index(n)
        return self.y_next(self.here(1, n), self.came_y(216 + 36 * slot, 36))

    def z_face(self, n):
        slot = (0, 1, 3).index(n)
        return self.zf[Z_L + 9 * slot : Z_L + 9 * slot + 9, :]

    def insertion_next(self, base, h, n, m):
        if m == 0:
            self.put(base, h, x_next(self.here(m, n)))
        elif m == 1:
            self.put(base, h, self.from_y(n))
        elif m == 2:
            self.put_z(base, h, self.here(m, n), self.z_face(n))
        else:
            self.put(base, h, self.from_t(n))

    def corner(self, base, h, m, n):
        if m == 0 and n == 1:
            self.put(base, h, x_next(self.from_y(0)))
        elif m == 0 and n == 2:
            self.put_z(base, h, x_next(self.here(0, 2)), x_next(self.z_face(0)))
        elif m == 0:
            self.put(base, h, x_next(self.from_t(0)))
        elif m == 1 and n == 2:
            face = self.z_face(1)
            came = self.zf[Z_ROWS + 16 : Z_ROWS + 25, :]
            self.put_z(base, h, self.from_y(2), jnp.where(low_half(face), roll64(face), came))
        elif m == 1:
            self.put(base, h, self.y_next(self.from_t(1), roll64(self.yf[Y_ROWS : Y_ROWS + 36, :])))
        else:
            self.put_z(base, h, self.from_t(2), self.zf[Z_ROWS : Z_ROWS + 9, :])

    def stage(self, base, pair):
        for h in range(2):
            m, n = pair[h]
            self.put(base + G_UM, h, self.link(m))
            self.put(base + G_UN, h, self.link(n))
            self.link_next(base + G_UN1, h, n, m)
            self.link_next(base + G_UM1, h, m, n)
            self.insertion_next(base + G_LM, h, n, m)
            self.insertion_next(base + G_LN, h, m, n)
            self.corner(base + G_LMN, h, m, n)
            self.put(base + G_L0, h, self.here(m, n))


def plane_force(geo, g, work, acc, a):
    um, un = full(geo, g + G_UM), full(geo, g + G_UN)
    un1, um1 = full(geo, g + G_UN1), full(geo, g + G_UM1)
    lm, ln, lmn, l0 = (herm(geo, g + k) for k in (G_LM, G_LN, G_LMN, G_L0))
    loop = keep(work, 0, product(un1, dagger(um1)))
    inner = keep(work, 144, product(un1, lmn))
    first = product(lm, loop)
    inner = keep(work, 288, product(inner, dagger(um1), first))
    inner = keep(work, 144, product(loop, ln, inner))
    inner = keep(work, 288, product(um, inner))
    loop = keep(work, 144, product(um, loop))
    whole = keep(work, 0, product(loop, dagger(un)))
    common = anti(inner, dagger(un))
    to_m = anti(whole, l0)
    to_n = anti(l0, whole)
    for e in range(9):
        scale = 0.5 if e < 3 else 0.25
        acc[pl.ds(a + 8 * e, 8), :] = scale * (common[e] + to_m[e])
        acc[pl.ds(a + 72 + 8 * e, 8), :] = scale * (common[e] + to_n[e])


def xy_kernel(xs, ys, weights, y_ref, hop, yf, far, near):
    yf[...] = y_ref[0:Y_REST, :].astype(F32)
    for index, value in far_halves(xs, ys, 0):
        far[8 * index : 8 * index + 8, :] = x_next(value)
    stage_near(xs, ys, weights, near, 0, 0)
    low = lane_index() < CX
    for index, value in far_halves(xs, ys, 1):
        row = 384 + 8 * index
        came = yf[8 * (index % 24) : 8 * (index % 24) + 8, :]
        if index < 24:
            far[row : row + 8, :] = roll64(jnp.where(low, came, value))
        else:
            far[row : row + 8, :] = jnp.where(low, roll64(value), came)
    stage_near(xs, ys, weights, near, 384, 1)

    def one_hop(m, carry):
        base = pl.multiple_of(m * 384, 8)
        hop_sums(far, near, base, base, hop, pl.multiple_of(m * 144, 8))
        return carry

    lax.fori_loop(0, 2, one_hop, 0)


def t_kernel(xs, ys, us, ld, weights, tl_ref, t_ref, y_ref, hop, acc, tl, tf, yf, near, geo, work):
    tl[...] = tl_ref[...].astype(F32)
    tf[...] = t_ref[T_LINK:T_ROWS, :].astype(F32)
    yf[...] = y_ref[...].astype(F32)
    geo[920:1304, :] = t_ref[0:384, :].astype(F32)
    stage_near(xs, ys, weights, near, 0, 3)
    hop_sums(geo, near, 920, 0, hop, 0)
    Neighbours(geo, us, ld, tf, tl, yf).stage(0, T_PAIR)
    plane_force(geo, 0, work, acc, 0)


def last_kernel(
    xs, ys, us, ld, weights, tl_ref, t_ref, y_ref, z_ref, hop_xy, hop_t, acc_t, out,
    tl, tf, yf, zf, far, near, hop, geo, work, acc,
):
    tl[...] = tl_ref[...].astype(F32)
    tf[...] = t_ref[T_LINK:T_ROWS, :].astype(F32)
    yf[...] = y_ref[...].astype(F32)
    zf[...] = z_ref[0 : Z_ROWS + 32, :].astype(F32)
    for index, value in far_halves(xs, ys, 2):
        far[8 + 8 * index - 2 : 8 + 8 * index + 6, :] = value
    far[pl.ds(8 + 6, 48, stride=8), :] = zf[0:48, :]
    far[pl.ds(8 + 7, 48, stride=8), :] = zf[48:96, :]
    stage_near(xs, ys, weights, near, 0, 2)
    hop_sums(far, near, 8, 0, hop, 0)
    places = Neighbours(geo, us, ld, tf, tl, yf, zf)
    for pair in range(2):
        places.stage(G_ROWS * pair, Z_PAIRS[pair])

    def one_pair(pair, carry):
        plane_force(geo, pl.multiple_of(pair * G_ROWS, 8), work, acc, pl.multiple_of(pair * 144, 8))
        return carry

    lax.fori_loop(0, 2, one_pair, 0)
    acc[288:432, :] = acc_t[...]

    even = lax.broadcasted_iota(jnp.int32, (8, LANES), 0) % 2 == 0
    places.put(0, 0, places.link(0))
    places.put(0, 1, places.link(1))
    places.put(144, 0, places.link(2))
    places.put(144, 1, places.link(3))
    halves = [((hop_xy, 0), (hop_xy, 144)), ((hop, 0), (hop_t, 0))]
    for pair in range(2):
        table = {}
        for ri in range(2):
            for c in range(3):
                for d in range(3):
                    row = 8 * (ri * 9 + c * 3 + d)
                    a, b = (ref[base + row : base + row + 8, :] for ref, base in halves[pair])
                    table[ri, c, d] = jnp.where(even, a + pltpu.roll(a, 7, 0), b + pltpu.roll(b, 1, 0))
        entries = anti(full(geo, 144 * pair), lambda ri, c, d: table[ri, c, d])
        for e in range(9):
            row = 432 + 72 * pair + 8 * e
            acc[row : row + 8, :] = entries[e] if e < 3 else 0.5 * entries[e]

    sources = [
        [(0, 0), (2, 0), (4, 0), (6, 0)],
        [(0, 1), (3, 0), (4, 1), (6, 1)],
        [(1, 0), (1, 1), (2, 1), (7, 0)],
        [(3, 1), (5, 0), (5, 1), (7, 1)],
    ]
    zero = jnp.zeros((4, LANES), F32)
    for m in range(4):
        values = []
        for e in range(9):
            total = None
            for slot, h in sources[m]:
                piece = acc[pl.ds(72 * slot + 8 * e + h, 4, stride=2), :]
                total = piece if total is None else total + piece
            values.append(total)
        trace = (values[0] + values[1] + values[2]) * (1.0 / 3.0)
        for c in range(3):
            for d in range(3):
                if c == d:
                    re, im = zero, values[c] - trace
                else:
                    e = 3 + 2 * OFF.index((min(c, d), max(c, d)))
                    re, im = (values[e] if c < d else -values[e]), values[e + 1]
                row = 72 * m + 4 * (3 * c + d)
                out[row : row + 4, :] = re
                out[row + 36 : row + 40, :] = im


def vmem(rows):
    return pltpu.VMEM((rows, LANES), F32)


IN_VMEM = pl.BlockSpec(memory_space=pltpu.VMEM)


def call(kernel, name, in_specs, outs, scratch, flops, out_specs=IN_VMEM):
    shapes = [jax.ShapeDtypeStruct((rows, LANES), kind) for rows, kind in outs]
    return pl.pallas_call(
        kernel,
        out_shape=shapes,
        in_specs=in_specs,
        out_specs=[out_specs] * len(shapes),
        scratch_shapes=[vmem(k) if isinstance(k, int) else k for k in scratch],
        compiler_params=pltpu.CompilerParams(vmem_limit_bytes=24 * 1024 * 1024),
        cost_estimate=pl.CostEstimate(flops=flops, bytes_accessed=1000000, transcendentals=0),
        name=name,
    )


def passed_back(block, *axes):
    sizes = [lax.axis_size(axis) for axis in axes]
    route = []
    for place in np.ndindex(*sizes):
        source = [(k + 1) % size for k, size in zip(place, sizes)]
        route.append((int(np.ravel_multi_index(source, sizes)), int(np.ravel_multi_index(place, sizes))))
    return lax.ppermute(block, axes if len(axes) > 1 else axes[0], route)


def shards(solution_x, solution_y, links, pole_coef):
    inputs = [solution_x.reshape(384, LANES), solution_y.reshape(384, LANES), links.reshape(288, LANES), pole_coef]
    xs, ys, us, local, weights, to_tl = call(
        first_kernel,
        "insertions",
        [pl.BlockSpec(memory_space=pltpu.HBM)] * 4,
        [(384, F32), (384, F32), (U_ROWS, F32), (LD_ROWS, F32), (16, F32), (L_ROWS, BF16)],
        [pltpu.VMEM((384, LANES), BF16)] * 2
        + [pltpu.VMEM((288, LANES), BF16), pltpu.SMEM((4,), F32), 432, L_ROWS, pltpu.SemaphoreType.DMA((4,))],
        1000000,
    )(*[pltpu.with_memory_space_constraint(array, pltpu.HBM) for array in inputs])
    tl_came = passed_back(to_tl, "ta")
    (to_t,) = call(t_pack_kernel, "pack_t", [IN_VMEM] * 3, [(T_ROWS, BF16)], [T_ROWS], 500000)(xs, ys, us)
    t_came = passed_back(to_t, "ta")
    (to_y,) = call(y_pack_kernel, "pack_y", [IN_VMEM] * 4, [(Y_ROWS, BF16)], [384, 336, Y_ROWS], 500000)(xs, ys, us, local)
    y_came = passed_back(jnp.concatenate([to_y, tl_came[0:48]]), "gy")
    (to_z,) = call(z_pack_kernel, "pack_z", [IN_VMEM] * 5, [(Z_ROWS + 16, BF16)], [384, Z_ROWS + 16], 500000)(
        xs, ys, us, local, tl_came
    )
    z_block = jnp.concatenate(
        [to_z, y_came[Y_CORNER : Y_CORNER + 16], t_came[T_ROWS - 16 :]]
    )
    z_came = passed_back(z_block, "gz")
    (hop_xy,) = call(
        xy_kernel, "hop_xy", [IN_VMEM] * 4, [(288, F32)], [Y_REST, 768, 768], 2000000
    )(xs, ys, weights, y_came)
    hop_t, acc_t = call(
        t_kernel,
        "force_t",
        [IN_VMEM] * 8,
        [(144, F32), (144, F32)],
        [L_ROWS, T_ROWS - T_LINK, Y_ROWS + 48, 384, 1304, 432],
        2000000,
    )(xs, ys, us, local, weights, tl_came, t_came, y_came)
    (force,) = call(
        last_kernel,
        "force",
        [IN_VMEM] * 12,
        [(288, F32)],
        [L_ROWS, T_ROWS - T_LINK, Y_ROWS + 48, Z_ROWS + 32, 400, 384, 144, 2 * G_ROWS, 432, 592],
        4000000,
        out_specs=pl.BlockSpec(),
    )(xs, ys, us, local, weights, tl_came, t_came, y_came, z_came, hop_xy, hop_t, acc_t)
    return force.reshape(links.shape)


def solution(mesh):
    placed = P(None, None, "ta", "gz", "gy")
    return jax.shard_map(
        shards, mesh=mesh, in_specs=(placed, placed, placed, P()), out_specs=placed, check_vma=False
    )
```

```python
import jax
import jax.numpy as jnp
import numpy as np
from jax import lax
from jax.experimental import pallas as pl
from jax.experimental.pallas import tpu as pltpu
from jax.sharding import PartitionSpec as P

F32, BF16 = jnp.float32, jnp.bfloat16
LANES, CX = 128, 64
PLANES = [(0, 1), (0, 2), (0, 3), (1, 2), (1, 3), (2, 3)]
T_PAIR = ((0, 3), (1, 3))
Z_PAIRS = [((0, 2), (1, 2)), ((0, 1), (2, 3))]
OFF = [(0, 1), (0, 2), (1, 2)]

U_ROWS, LD_ROWS = 320, 256

L_XT, L_ZT, L_CORNER, L_ROWS = 48, 84, 128, 144
T_LINK, T_ROWS = 384, 608
Y_REST, Y_HALF, Y_CORNER, Y_ROWS = 192, 168, 360, 384
Z_LINK, Z_L, Z_CORNER, Z_ROWS = 96, 150, 177, 192

G_UN1, G_UM1 = 8, 160
G_LM, G_LN, G_LMN, G_L0 = 312, 392, 472, 552
G_UM, G_UN = 624, 768
G_ROWS = 920


def spin_tables():
    one = np.array([[0, 1], [1, 0]], dtype=complex)
    two = np.array([[0, -1j], [1j, 0]], dtype=complex)
    three = np.array([[1, 0], [0, -1]], dtype=complex)
    pauli = [one, two, three]
    blocks = [-1j * one, -1j * two, -1j * three, np.eye(2, dtype=complex)]
    insert = []
    for m, n in PLANES:
        b, c = blocks[m], blocks[n]
        up = 0.5j * (b @ c.conj().T - c @ b.conj().T)
        low = 0.5j * (b.conj().T @ c - c.conj().T @ b)
        entry = []
        for block in (up, low):
            for j in range(3):
                sign = np.trace(block @ pauli[j]).real / 2
                if abs(sign) > 0.5:
                    entry.append((j, float(sign)))
        insert.append(entry)
    return blocks, insert


BLOCKS, INSERT = spin_tables()


def lane_index():
    return lax.broadcasted_iota(jnp.int32, (8, LANES), 1)


def roll64(v):
    return pltpu.roll(v, CX, 1)


def x_next(v):
    lanes = lax.broadcasted_iota(jnp.int32, v.shape, 1)
    return jnp.where(lanes % CX == CX - 1, pltpu.roll(v, CX - 1, 1), pltpu.roll(v, LANES - 1, 1))


def low_half(v):
    return lax.broadcasted_iota(jnp.int32, v.shape, 1) < CX


def pair_spinors(src, base, dst):
    for k in range(4):
        dst[pl.ds(192 * (k % 2) + k // 2, 96, stride=2), :] = src[base + 96 * k : base + 96 * k + 96, :].astype(F32)


def spin_part(ref, p, ri, spin, col):
    row = 192 * p + 8 * (ri * 12 + spin * 3 + col)
    return ref[row : row + 8, :]


def half_component(ref, p, ri, spin, col, m, sign):
    base = spin_part(ref, p, ri, spin, col)
    for b in range(2):
        coeff = sign * BLOCKS[m][spin, b]
        if coeff.real != 0:
            low = spin_part(ref, p, ri, 2 + b, col)
            base = base + low if coeff.real > 0 else base - low
        if coeff.imag != 0:
            low = spin_part(ref, p, 1 - ri, 2 + b, col)
            positive = (coeff.imag > 0) == (ri == 1)
            base = base + low if positive else base - low
    return base


def far_halves(xs, ys, m):
    for p in range(2):
        for term, (ref, sign) in enumerate(((xs, -1.0), (ys, 1.0))):
            for ri in range(2):
                for spin in range(2):
                    for col in range(3):
                        index = p * 24 + term * 12 + ri * 6 + spin * 3 + col
                        yield index, half_component(ref, p, ri, spin, col, m, sign)


def insertions(xs, ys, weights, ls, ld):
    matrices = []
    for chi in range(2):
        cross = {}
        third = {}

        def add(store, key, value):
            store[key] = value if key not in store else store[key] + value

        for p in range(2):
            w = weights[8 * p : 8 * p + 8, :]
            x = [[[spin_part(xs, p, ri, 2 * chi + s, c) for ri in range(2)] for c in range(3)] for s in range(2)]
            y = [[[spin_part(ys, p, ri, 2 * chi + s, c) * w for ri in range(2)] for c in range(3)] for s in range(2)]
            for c in range(3):
                for d in range(3):
                    for left, right in ((x, y), (y, x)):
                        a, b = left[1][c], right[0][d]
                        add(cross, (c, d, 0), a[0] * b[0] + a[1] * b[1])
                        add(cross, (c, d, 1), a[1] * b[0] - a[0] * b[1])
            for c in range(3):
                value = (x[0][c][0] * y[0][c][0] + x[0][c][1] * y[0][c][1]) - (
                    x[1][c][0] * y[1][c][0] + x[1][c][1] * y[1][c][1]
                )
                add(third, (c,), value)
            for c, d in OFF:
                for left, right in ((x, y), (y, x)):
                    for s in range(2):
                        a, b = left[s][c], right[s][d]
                        re = a[0] * b[0] + a[1] * b[1]
                        im = a[1] * b[0] - a[0] * b[1]
                        add(third, (c, d, 0), re if s == 0 else -re)
                        add(third, (c, d, 1), im if s == 0 else -im)
        first = [2.0 * cross[c, c, 0] for c in range(3)]
        second = [2.0 * cross[c, c, 1] for c in range(3)]
        last = [2.0 * third[(c,)] for c in range(3)]
        for c, d in OFF:
            first += [cross[c, d, 0] + cross[d, c, 0], cross[c, d, 1] - cross[d, c, 1]]
            second += [cross[c, d, 1] + cross[d, c, 1], cross[d, c, 0] - cross[c, d, 0]]
            last += [third[c, d, 0], third[c, d, 1]]
        matrices.append((first, second, last))
    for plane in range(6):
        (up, up_sign), (low, low_sign) = INSERT[plane]
        for e in range(9):
            a, b = matrices[0][up][e], matrices[1][low][e]
            value = a + b if up_sign * low_sign > 0 else a - b
            row = (plane * 9 + e) * 8
            ls[row : row + 8, :] = value if up_sign > 0 else -value
    ld[0:216, :] = ls[pl.ds(0, 216, stride=2), :] + ls[pl.ds(1, 216, stride=2), :]


def plane_rows(m, n):
    base = 36 * PLANES.index((min(m, n), max(m, n)))
    return slice(base, base + 36)


def first_kernel(
    x_hbm, y_hbm, u_hbm, coef_hbm, xs, ys, us, ld, weights, tl_out,
    x_ref, y_ref, u_ref, coef, ls, ds, sems,
):
    pairs = ((coef_hbm, coef), (x_hbm, x_ref), (y_hbm, y_ref), (u_hbm, u_ref))
    copies = [pltpu.make_async_copy(source, target, sems.at[k]) for k, (source, target) in enumerate(pairs)]
    for copy in copies:
        copy.start()
    copies[1].wait()
    pair_spinors(x_ref, 0, xs)
    copies[2].wait()
    pair_spinors(y_ref, 0, ys)
    copies[0].wait()
    even = lax.broadcasted_iota(jnp.int32, (8, LANES), 0) % 2 == 0
    for p in range(2):
        weights[8 * p : 8 * p + 8, :] = jnp.where(even, coef[p], coef[p + 2])
    insertions(xs, ys, weights, ls, ld)
    copies[3].wait()
    us[0:288, :] = u_ref[...].astype(F32)
    ds[...] = jnp.zeros((L_ROWS, LANES), F32)
    ds[0:36, :] = ld[plane_rows(1, 3), :]
    ds[L_XT : L_XT + 36, :] = ld[plane_rows(0, 3), :]
    ds[L_ZT : L_ZT + 36, :] = ld[plane_rows(2, 3), :]
    ds[L_CORNER : L_CORNER + 9, :] = ld[pl.ds(plane_rows(2, 3).start, 9, stride=4), :]
    tl_out[...] = ds[...].astype(BF16)


def y_pack_kernel(xs, ys, us, ld, y_out, hs, ds, ys2):
    for index, value in far_halves(xs, ys, 1):
        hs[8 * index : 8 * index + 8, :] = value
    first, second = hs[0:192, :], hs[192:384, :]
    ys2[0:192, :] = jnp.where(low_half(first), first, roll64(second))
    for slot, n in enumerate((0, 2, 3)):
        ds[72 * slot : 72 * slot + 72, :] = us[72 * n : 72 * n + 72, :]
        ds[216 + 36 * slot : 216 + 36 * slot + 36, :] = ld[plane_rows(1, n), :]
    ds[324:336, :] = jnp.zeros((12, LANES), F32)
    first, second = ds[0:Y_HALF, :], ds[Y_HALF : 2 * Y_HALF, :]
    ys2[Y_REST : Y_REST + Y_HALF, :] = jnp.where(low_half(first), first, roll64(second))
    ys2[Y_CORNER:Y_ROWS, :] = jnp.zeros((Y_ROWS - Y_CORNER, LANES), F32)
    ys2[Y_CORNER : Y_CORNER + 9, :] = roll64(ld[pl.ds(plane_rows(1, 2).start, 9, stride=4), :])
    y_out[...] = ys2[...].astype(BF16)


def t_pack_kernel(xs, ys, us, t_out, ts):
    for index, value in far_halves(xs, ys, 3):
        ts[8 * index : 8 * index + 8, :] = value
    ts[T_LINK : T_LINK + 216, :] = us[0:216, :]
    ts[T_LINK + 216 : T_ROWS, :] = jnp.zeros((T_ROWS - T_LINK - 216, LANES), F32)
    t_out[...] = ts[...].astype(BF16)


def z_pack_kernel(xs, ys, us, ld, tl_ref, z_out, hs, zs):
    for index, value in far_halves(xs, ys, 2):
        hs[8 * index : 8 * index + 8, :] = value
    zs[0:48, :] = hs[pl.ds(0, 48, stride=8), :]
    zs[48:96, :] = hs[pl.ds(1, 48, stride=8), :]
    for slot, n in enumerate((0, 1, 3)):
        zs[Z_LINK + 18 * slot : Z_LINK + 18 * slot + 18, :] = us[pl.ds(72 * n, 18, stride=4), :]
        zs[Z_L + 9 * slot : Z_L + 9 * slot + 9, :] = ld[pl.ds(plane_rows(2, n).start, 9, stride=4), :]
    zs[Z_L + 27 : Z_ROWS, :] = jnp.zeros((Z_ROWS - Z_L - 27, LANES), F32)
    zs[Z_CORNER : Z_CORNER + 9, :] = tl_ref[L_CORNER:L_ROWS, :].astype(F32)[0:9, :]
    z_out[...] = zs[...].astype(BF16)


def full(ref, base):
    def get(ri, c, d):
        return ref[pl.ds(base + 8 * (ri * 9 + c * 3 + d), 8), :]

    return get


def herm(ref, base):
    def get(ri, c, d):
        if c == d:
            return None if ri else ref[pl.ds(base + 8 * c, 8), :]
        low, high = min(c, d), max(c, d)
        value = ref[pl.ds(base + 8 * (3 + 2 * OFF.index((low, high)) + ri), 8), :]
        return -value if ri and c > d else value

    return get


def dagger(get):
    def other(ri, c, d):
        value = get(ri, d, c)
        return -value if ri and value is not None else value

    return other


def dot(left, right, ri, c, d):
    total = None
    for e in range(3):
        for part in range(2):
            a, b = left(part, c, e), right(ri ^ part, e, d)
            if a is None or b is None:
                continue
            term = a * b
            if ri == 0 and part == 1:
                total = -term if total is None else total - term
            else:
                total = term if total is None else total + term
    return total


def held(get):
    table = {(ri, c, d): get(ri, c, d) for ri in range(2) for c in range(3) for d in range(3)}
    return lambda ri, c, d: table[ri, c, d]


def product(left, right, extra=None):
    table = {}
    for c in range(3):
        for d in range(3):
            for ri in range(2):
                value = dot(left, right, ri, c, d)
                if extra is not None:
                    value = value + extra(ri, c, d)
                table[ri, c, d] = value
    return lambda ri, c, d: table[ri, c, d]


def keep(ref, base, get):
    for ri in range(2):
        for c in range(3):
            for d in range(3):
                ref[pl.ds(base + 8 * (ri * 9 + c * 3 + d), 8), :] = get(ri, c, d)
    return full(ref, base)


def anti(left, right):
    entries = [dot(left, right, 1, c, c) for c in range(3)]
    for c, d in OFF:
        entries.append(dot(left, right, 0, c, d) - dot(left, right, 0, d, c))
        entries.append(dot(left, right, 1, c, d) + dot(left, right, 1, d, c))
    return entries


def stage_near(xs, ys, weights, near, base, m):
    for p in range(2):
        for term, (ref, sign) in enumerate(((ys, -1.0), (xs, 1.0))):
            for ri in range(2):
                for spin in range(2):
                    for col in range(3):
                        index = p * 24 + term * 12 + ri * 6 + spin * 3 + col
                        row = base + 8 * index
                        near[row : row + 8, :] = half_component(ref, p, ri, spin, col, m, sign) * weights[8 * p : 8 * p + 8, :]


def hop_sums(far, near, far_base, near_base, hop, hop_base):
    sums = {}
    for p in range(2):
        for term in range(2):
            for spin in range(2):

                def part(ref, base, ri, col):
                    return ref[pl.ds(base + 8 * (p * 24 + term * 12 + ri * 6 + spin * 3 + col), 8), :]

                a = [[part(far, far_base, ri, c) for ri in range(2)] for c in range(3)]
                b = [[part(near, near_base, ri, c) for ri in range(2)] for c in range(3)]
                for c in range(3):
                    for d in range(3):
                        re = a[c][0] * b[d][0] + a[c][1] * b[d][1]
                        im = a[c][1] * b[d][0] - a[c][0] * b[d][1]
                        if (c, d) in sums:
                            sums[c, d] = (sums[c, d][0] + re, sums[c, d][1] + im)
                        else:
                            sums[c, d] = (re, im)
    for c in range(3):
        for d in range(3):
            for ri in range(2):
                hop[pl.ds(hop_base + 8 * (ri * 9 + c * 3 + d), 8), :] = sums[c, d][ri]


class Neighbours:
    def __init__(self, geo, us, ld, tf=None, tl=None, yf=None, zf=None):
        self.geo, self.us, self.ld, self.tf, self.tl, self.yf, self.zf = geo, us, ld, tf, tl, yf, zf

    def link(self, n):
        return self.us[72 * n : 72 * n + 72, :]

    def came_y(self, row, count):
        pieces = []
        if row < Y_HALF:
            stop = min(row + count, Y_HALF)
            pieces.append(roll64(self.yf[Y_REST + row : Y_REST + stop, :]))
            count, row = count - (stop - row), stop
        if count:
            pieces.append(self.yf[Y_REST + row - Y_HALF : Y_REST + row - Y_HALF + count, :])
        return pieces[0] if len(pieces) == 1 else jnp.concatenate(pieces, axis=0)

    def y_next(self, here, came):
        return jnp.where(low_half(here), roll64(here), came)

    def put(self, base, h, value):
        self.geo[pl.ds(base + h, value.shape[0], stride=2), :] = value

    def put_z(self, base, h, value, face):
        self.geo[pl.ds(base + h - 2, value.shape[0], stride=2), :] = value
        self.geo[pl.ds(base + h + 6, face.shape[0], stride=8), :] = face

    def link_next(self, base, h, n, m):
        slot = [k for k in range(4) if k != m].index(n)
        if m == 0:
            self.put(base, h, x_next(self.link(n)))
        elif m == 1:
            self.put(base, h, self.y_next(self.link(n), self.came_y(72 * slot, 72)))
        elif m == 2:
            self.put_z(base, h, self.link(n), self.zf[Z_LINK + 18 * slot : Z_LINK + 18 * slot + 18, :])
        else:
            self.put(base, h, self.tf[72 * slot : 72 * slot + 72, :])

    def here(self, m, n):
        return self.ld[plane_rows(m, n), :]

    def from_t(self, n):
        row = (L_XT, 0, L_ZT)[n]
        return self.tl[row : row + 36, :]

    def from_y(self, n):
        slot = (0, 2, 3).index(n)
        return self.y_next(self.here(1, n), self.came_y(216 + 36 * slot, 36))

    def z_face(self, n):
        slot = (0, 1, 3).index(n)
        return self.zf[Z_L + 9 * slot : Z_L + 9 * slot + 9, :]

    def insertion_next(self, base, h, n, m):
        if m == 0:
            self.put(base, h, x_next(self.here(m, n)))
        elif m == 1:
            self.put(base, h, self.from_y(n))
        elif m == 2:
            self.put_z(base, h, self.here(m, n), self.z_face(n))
        else:
            self.put(base, h, self.from_t(n))

    def corner(self, base, h, m, n):
        if m == 0 and n == 1:
            self.put(base, h, x_next(self.from_y(0)))
        elif m == 0 and n == 2:
            self.put_z(base, h, x_next(self.here(0, 2)), x_next(self.z_face(0)))
        elif m == 0:
            self.put(base, h, x_next(self.from_t(0)))
        elif m == 1 and n == 2:
            face = self.z_face(1)
            came = self.zf[Z_ROWS : Z_ROWS + 9, :]
            self.put_z(base, h, self.from_y(2), jnp.where(low_half(face), roll64(face), came))
        elif m == 1:
            self.put(base, h, self.y_next(self.from_t(1), roll64(self.yf[Y_ROWS : Y_ROWS + 36, :])))
        else:
            self.put_z(base, h, self.from_t(2), self.zf[Z_CORNER : Z_CORNER + 9, :])

    def stage(self, base, pair):
        for h in range(2):
            m, n = pair[h]
            self.put(base + G_UM, h, self.link(m))
            self.put(base + G_UN, h, self.link(n))
            self.link_next(base + G_UN1, h, n, m)
            self.link_next(base + G_UM1, h, m, n)
            self.insertion_next(base + G_LM, h, n, m)
            self.insertion_next(base + G_LN, h, m, n)
            self.corner(base + G_LMN, h, m, n)
            self.put(base + G_L0, h, self.here(m, n))


def plane_force(geo, g, work, acc, a):
    um, un = full(geo, g + G_UM), full(geo, g + G_UN)
    un1, um1 = full(geo, g + G_UN1), full(geo, g + G_UM1)
    lm, ln, lmn, l0 = (herm(geo, g + k) for k in (G_LM, G_LN, G_LMN, G_L0))
    loop = keep(work, 0, product(un1, dagger(um1)))
    inner = keep(work, 144, product(un1, lmn))
    first = product(lm, loop)
    inner = keep(work, 288, product(inner, dagger(um1), first))
    inner = keep(work, 144, product(loop, ln, inner))
    inner = keep(work, 288, product(um, inner))
    loop = keep(work, 144, product(um, loop))
    whole = keep(work, 0, product(loop, dagger(un)))
    common = anti(inner, dagger(un))
    to_m = anti(whole, l0)
    to_n = anti(l0, whole)
    for e in range(9):
        scale = 0.5 if e < 3 else 0.25
        acc[pl.ds(a + 8 * e, 8), :] = scale * (common[e] + to_m[e])
        acc[pl.ds(a + 72 + 8 * e, 8), :] = scale * (common[e] + to_n[e])


def xy_kernel(xs, ys, weights, y_ref, hop, yf, far, near):
    yf[...] = y_ref[0:Y_REST, :].astype(F32)
    for index, value in far_halves(xs, ys, 0):
        far[8 * index : 8 * index + 8, :] = x_next(value)
    stage_near(xs, ys, weights, near, 0, 0)
    low = lane_index() < CX
    for index, value in far_halves(xs, ys, 1):
        row = 384 + 8 * index
        came = yf[8 * (index % 24) : 8 * (index % 24) + 8, :]
        if index < 24:
            far[row : row + 8, :] = roll64(jnp.where(low, came, value))
        else:
            far[row : row + 8, :] = jnp.where(low, roll64(value), came)
    stage_near(xs, ys, weights, near, 384, 1)

    def one_hop(m, carry):
        base = pl.multiple_of(m * 384, 8)
        hop_sums(far, near, base, base, hop, pl.multiple_of(m * 144, 8))
        return carry

    lax.fori_loop(0, 2, one_hop, 0)


def t_kernel(xs, ys, us, ld, weights, tl_ref, t_ref, y_ref, hop, acc, tl, tf, yf, near, geo, work):
    tl[...] = tl_ref[...].astype(F32)
    tf[...] = t_ref[T_LINK:T_ROWS, :].astype(F32)
    yf[...] = y_ref[...].astype(F32)
    geo[920:1304, :] = t_ref[0:384, :].astype(F32)
    stage_near(xs, ys, weights, near, 0, 3)
    hop_sums(geo, near, 920, 0, hop, 0)
    Neighbours(geo, us, ld, tf, tl, yf).stage(0, T_PAIR)
    plane_force(geo, 0, work, acc, 0)


def last_kernel(
    xs, ys, us, ld, weights, tl_ref, t_ref, y_ref, z_ref, hop_xy, hop_t, acc_t, out,
    tl, tf, yf, zf, far, near, hop, geo, work, acc,
):
    tl[...] = tl_ref[...].astype(F32)
    tf[...] = t_ref[T_LINK:T_ROWS, :].astype(F32)
    yf[...] = y_ref[...].astype(F32)
    zf[...] = z_ref[0 : Z_ROWS + 16, :].astype(F32)
    for index, value in far_halves(xs, ys, 2):
        far[8 + 8 * index - 2 : 8 + 8 * index + 6, :] = value
    far[pl.ds(8 + 6, 48, stride=8), :] = zf[0:48, :]
    far[pl.ds(8 + 7, 48, stride=8), :] = zf[48:96, :]
    stage_near(xs, ys, weights, near, 0, 2)
    hop_sums(far, near, 8, 0, hop, 0)
    places = Neighbours(geo, us, ld, tf, tl, yf, zf)
    for pair in range(2):
        places.stage(G_ROWS * pair, Z_PAIRS[pair])

    def one_pair(pair, carry):
        plane_force(geo, pl.multiple_of(pair * G_ROWS, 8), work, acc, pl.multiple_of(pair * 144, 8))
        return carry

    lax.fori_loop(0, 2, one_pair, 0)
    acc[288:432, :] = acc_t[...]

    even = lax.broadcasted_iota(jnp.int32, (8, LANES), 0) % 2 == 0
    places.put(0, 0, places.link(0))
    places.put(0, 1, places.link(1))
    places.put(144, 0, places.link(2))
    places.put(144, 1, places.link(3))
    halves = [((hop_xy, 0), (hop_xy, 144)), ((hop, 0), (hop_t, 0))]
    for pair in range(2):
        table = {}
        for ri in range(2):
            for c in range(3):
                for d in range(3):
                    row = 8 * (ri * 9 + c * 3 + d)
                    a, b = (ref[base + row : base + row + 8, :] for ref, base in halves[pair])
                    table[ri, c, d] = jnp.where(even, a + pltpu.roll(a, 7, 0), b + pltpu.roll(b, 1, 0))
        entries = anti(full(geo, 144 * pair), lambda ri, c, d: table[ri, c, d])
        for e in range(9):
            row = 432 + 72 * pair + 8 * e
            acc[row : row + 8, :] = entries[e] if e < 3 else 0.5 * entries[e]

    sources = [
        [(0, 0), (2, 0), (4, 0), (6, 0)],
        [(0, 1), (3, 0), (4, 1), (6, 1)],
        [(1, 0), (1, 1), (2, 1), (7, 0)],
        [(3, 1), (5, 0), (5, 1), (7, 1)],
    ]
    zero = jnp.zeros((4, LANES), F32)
    for m in range(4):
        values = []
        for e in range(9):
            total = None
            for slot, h in sources[m]:
                piece = acc[pl.ds(72 * slot + 8 * e + h, 4, stride=2), :]
                total = piece if total is None else total + piece
            values.append(total)
        trace = (values[0] + values[1] + values[2]) * (1.0 / 3.0)
        for c in range(3):
            for d in range(3):
                if c == d:
                    re, im = zero, values[c] - trace
                else:
                    e = 3 + 2 * OFF.index((min(c, d), max(c, d)))
                    re, im = (values[e] if c < d else -values[e]), values[e + 1]
                row = 72 * m + 4 * (3 * c + d)
                out[row : row + 4, :] = re
                out[row + 36 : row + 40, :] = im


def vmem(rows):
    return pltpu.VMEM((rows, LANES), F32)


IN_VMEM = pl.BlockSpec(memory_space=pltpu.VMEM)


def call(kernel, name, in_specs, outs, scratch, flops, out_specs=IN_VMEM):
    shapes = [jax.ShapeDtypeStruct((rows, LANES), kind) for rows, kind in outs]
    return pl.pallas_call(
        kernel,
        out_shape=shapes,
        in_specs=in_specs,
        out_specs=[out_specs] * len(shapes),
        scratch_shapes=[vmem(k) if isinstance(k, int) else k for k in scratch],
        compiler_params=pltpu.CompilerParams(vmem_limit_bytes=24 * 1024 * 1024),
        cost_estimate=pl.CostEstimate(flops=flops, bytes_accessed=1000000, transcendentals=0),
        name=name,
    )


def passed_back(block, *axes):
    sizes = [lax.axis_size(axis) for axis in axes]
    route = []
    for place in np.ndindex(*sizes):
        source = [(k + 1) % size for k, size in zip(place, sizes)]
        route.append((int(np.ravel_multi_index(source, sizes)), int(np.ravel_multi_index(place, sizes))))
    return lax.ppermute(block, axes if len(axes) > 1 else axes[0], route)


def shards(solution_x, solution_y, links, pole_coef):
    inputs = [solution_x.reshape(384, LANES), solution_y.reshape(384, LANES), links.reshape(288, LANES), pole_coef]
    xs, ys, us, local, weights, to_tl = call(
        first_kernel,
        "insertions",
        [pl.BlockSpec(memory_space=pltpu.HBM)] * 4,
        [(384, F32), (384, F32), (U_ROWS, F32), (LD_ROWS, F32), (16, F32), (L_ROWS, BF16)],
        [pltpu.VMEM((384, LANES), BF16)] * 2
        + [pltpu.VMEM((288, LANES), BF16), pltpu.SMEM((4,), F32), 432, L_ROWS, pltpu.SemaphoreType.DMA((4,))],
        1000000,
    )(*[pltpu.with_memory_space_constraint(array, pltpu.HBM) for array in inputs])
    tl_came = passed_back(to_tl, "ta")
    (to_t,) = call(t_pack_kernel, "pack_t", [IN_VMEM] * 3, [(T_ROWS, BF16)], [T_ROWS], 500000)(xs, ys, us)
    t_came = passed_back(to_t, "ta")
    (to_y,) = call(y_pack_kernel, "pack_y", [IN_VMEM] * 4, [(Y_ROWS, BF16)], [384, 336, Y_ROWS], 500000)(xs, ys, us, local)
    y_came = passed_back(jnp.concatenate([to_y, tl_came[0:48]]), "gy")
    (to_z,) = call(z_pack_kernel, "pack_z", [IN_VMEM] * 5, [(Z_ROWS, BF16)], [384, Z_ROWS], 500000)(
        xs, ys, us, local, tl_came
    )
    z_block = jnp.concatenate(
        [to_z, y_came[Y_CORNER : Y_CORNER + 16], t_came[T_ROWS - 16 :]]
    )
    z_came = passed_back(z_block, "gz")
    (hop_xy,) = call(
        xy_kernel, "hop_xy", [IN_VMEM] * 4, [(288, F32)], [Y_REST, 768, 768], 2000000
    )(xs, ys, weights, y_came)
    hop_t, acc_t = call(
        t_kernel,
        "force_t",
        [IN_VMEM] * 8,
        [(144, F32), (144, F32)],
        [L_ROWS, T_ROWS - T_LINK, Y_ROWS + 48, 384, 1304, 432],
        2000000,
    )(xs, ys, us, local, weights, tl_came, t_came, y_came)
    (force,) = call(
        last_kernel,
        "force",
        [IN_VMEM] * 12,
        [(288, F32)],
        [L_ROWS, T_ROWS - T_LINK, Y_ROWS + 48, Z_ROWS + 16, 400, 384, 144, 2 * G_ROWS, 432, 592],
        4000000,
        out_specs=pl.BlockSpec(),
    )(xs, ys, us, local, weights, tl_came, t_came, y_came, z_came, hop_xy, hop_t, acc_t)
    return force.reshape(links.shape)


def solution(mesh):
    placed = P(None, None, "ta", "gz", "gy")
    return jax.shard_map(
        shards, mesh=mesh, in_specs=(placed, placed, placed, P()), out_specs=placed, check_vma=False
    )
```

```python
import jax
import jax.numpy as jnp
import numpy as np
from jax import lax
from jax.experimental import pallas as pl
from jax.experimental.pallas import tpu as pltpu
from jax.sharding import PartitionSpec as P

F32, BF16 = jnp.float32, jnp.bfloat16
LANES, CX = 128, 64
PLANES = [(0, 1), (0, 2), (0, 3), (1, 2), (1, 3), (2, 3)]
T_PAIR = ((0, 3), (1, 3))
Z_PAIRS = [((0, 2), (1, 2)), ((0, 1), (2, 3))]
OFF = [(0, 1), (0, 2), (1, 2)]

U_ROWS, LD_ROWS = 320, 256

L_XT, L_ZT, L_CORNER, L_ROWS = 48, 84, 128, 144
T_LINK, T_ROWS = 384, 608
Y_REST, Y_HALF, Y_CORNER, Y_ROWS = 192, 168, 360, 384
Z_LINK, Z_L, Z_CORNER, Z_ROWS = 96, 150, 177, 192

G_UN1, G_UM1 = 8, 160
G_LM, G_LN, G_LMN, G_L0 = 312, 392, 472, 552
G_UM, G_UN = 624, 768
G_ROWS = 920


def spin_tables():
    one = np.array([[0, 1], [1, 0]], dtype=complex)
    two = np.array([[0, -1j], [1j, 0]], dtype=complex)
    three = np.array([[1, 0], [0, -1]], dtype=complex)
    pauli = [one, two, three]
    blocks = [-1j * one, -1j * two, -1j * three, np.eye(2, dtype=complex)]
    insert = []
    for m, n in PLANES:
        b, c = blocks[m], blocks[n]
        up = 0.5j * (b @ c.conj().T - c @ b.conj().T)
        low = 0.5j * (b.conj().T @ c - c.conj().T @ b)
        entry = []
        for block in (up, low):
            for j in range(3):
                sign = np.trace(block @ pauli[j]).real / 2
                if abs(sign) > 0.5:
                    entry.append((j, float(sign)))
        insert.append(entry)
    return blocks, insert


BLOCKS, INSERT = spin_tables()


def lane_index():
    return lax.broadcasted_iota(jnp.int32, (8, LANES), 1)


def roll64(v):
    return pltpu.roll(v, CX, 1)


def x_next(v):
    lanes = lax.broadcasted_iota(jnp.int32, v.shape, 1)
    return jnp.where(lanes % CX == CX - 1, pltpu.roll(v, CX - 1, 1), pltpu.roll(v, LANES - 1, 1))


def low_half(v):
    return lax.broadcasted_iota(jnp.int32, v.shape, 1) < CX


def pair_spinors(src, base, dst):
    for k in range(4):
        dst[pl.ds(192 * (k % 2) + k // 2, 96, stride=2), :] = src[base + 96 * k : base + 96 * k + 96, :].astype(F32)


def spin_part(ref, p, ri, spin, col):
    row = 192 * p + 8 * (ri * 12 + spin * 3 + col)
    return ref[row : row + 8, :]


def half_component(ref, p, ri, spin, col, m, sign):
    base = spin_part(ref, p, ri, spin, col)
    for b in range(2):
        coeff = sign * BLOCKS[m][spin, b]
        if coeff.real != 0:
            low = spin_part(ref, p, ri, 2 + b, col)
            base = base + low if coeff.real > 0 else base - low
        if coeff.imag != 0:
            low = spin_part(ref, p, 1 - ri, 2 + b, col)
            positive = (coeff.imag > 0) == (ri == 1)
            base = base + low if positive else base - low
    return base


def far_halves(xs, ys, m):
    for p in range(2):
        for term, (ref, sign) in enumerate(((xs, -1.0), (ys, 1.0))):
            for ri in range(2):
                for spin in range(2):
                    for col in range(3):
                        index = p * 24 + term * 12 + ri * 6 + spin * 3 + col
                        yield index, half_component(ref, p, ri, spin, col, m, sign)


def insertions(xs, ys, weights, ls, ld):
    matrices = []
    for chi in range(2):
        cross = {}
        third = {}

        def add(store, key, value):
            store[key] = value if key not in store else store[key] + value

        for p in range(2):
            w = weights[8 * p : 8 * p + 8, :]
            x = [[[spin_part(xs, p, ri, 2 * chi + s, c) for ri in range(2)] for c in range(3)] for s in range(2)]
            y = [[[spin_part(ys, p, ri, 2 * chi + s, c) * w for ri in range(2)] for c in range(3)] for s in range(2)]
            for c in range(3):
                for d in range(3):
                    for left, right in ((x, y), (y, x)):
                        a, b = left[1][c], right[0][d]
                        add(cross, (c, d, 0), a[0] * b[0] + a[1] * b[1])
                        add(cross, (c, d, 1), a[1] * b[0] - a[0] * b[1])
            for c in range(3):
                value = (x[0][c][0] * y[0][c][0] + x[0][c][1] * y[0][c][1]) - (
                    x[1][c][0] * y[1][c][0] + x[1][c][1] * y[1][c][1]
                )
                add(third, (c,), value)
            for c, d in OFF:
                for left, right in ((x, y), (y, x)):
                    for s in range(2):
                        a, b = left[s][c], right[s][d]
                        re = a[0] * b[0] + a[1] * b[1]
                        im = a[1] * b[0] - a[0] * b[1]
                        add(third, (c, d, 0), re if s == 0 else -re)
                        add(third, (c, d, 1), im if s == 0 else -im)
        first = [2.0 * cross[c, c, 0] for c in range(3)]
        second = [2.0 * cross[c, c, 1] for c in range(3)]
        last = [2.0 * third[(c,)] for c in range(3)]
        for c, d in OFF:
            first += [cross[c, d, 0] + cross[d, c, 0], cross[c, d, 1] - cross[d, c, 1]]
            second += [cross[c, d, 1] + cross[d, c, 1], cross[d, c, 0] - cross[c, d, 0]]
            last += [third[c, d, 0], third[c, d, 1]]
        matrices.append((first, second, last))
    for plane in range(6):
        (up, up_sign), (low, low_sign) = INSERT[plane]
        for e in range(9):
            a, b = matrices[0][up][e], matrices[1][low][e]
            value = a + b if up_sign * low_sign > 0 else a - b
            row = (plane * 9 + e) * 8
            ls[row : row + 8, :] = value if up_sign > 0 else -value
    ld[0:216, :] = ls[pl.ds(0, 216, stride=2), :] + ls[pl.ds(1, 216, stride=2), :]


def plane_rows(m, n):
    base = 36 * PLANES.index((min(m, n), max(m, n)))
    return slice(base, base + 36)


def first_kernel(
    x_hbm, y_hbm, u_hbm, coef_hbm, xs, ys, us, ld, weights, tl_out,
    x_ref, y_ref, u_ref, coef, ls, ds, sems,
):
    pairs = ((coef_hbm, coef), (x_hbm, x_ref), (y_hbm, y_ref), (u_hbm, u_ref))
    copies = [pltpu.make_async_copy(source, target, sems.at[k]) for k, (source, target) in enumerate(pairs)]
    for copy in copies:
        copy.start()
    copies[1].wait()
    pair_spinors(x_ref, 0, xs)
    copies[2].wait()
    pair_spinors(y_ref, 0, ys)
    copies[0].wait()
    even = lax.broadcasted_iota(jnp.int32, (8, LANES), 0) % 2 == 0
    for p in range(2):
        weights[8 * p : 8 * p + 8, :] = jnp.where(even, coef[p], coef[p + 2])
    insertions(xs, ys, weights, ls, ld)
    copies[3].wait()
    us[0:288, :] = u_ref[...].astype(F32)
    ds[...] = jnp.zeros((L_ROWS, LANES), F32)
    ds[0:36, :] = ld[plane_rows(1, 3), :]
    ds[L_XT : L_XT + 36, :] = ld[plane_rows(0, 3), :]
    ds[L_ZT : L_ZT + 36, :] = ld[plane_rows(2, 3), :]
    ds[L_CORNER : L_CORNER + 9, :] = ld[pl.ds(plane_rows(2, 3).start, 9, stride=4), :]
    tl_out[...] = ds[...].astype(BF16)


def y_pack_kernel(xs, ys, us, ld, y_out, hs, ds, ys2):
    for index, value in far_halves(xs, ys, 1):
        hs[8 * index : 8 * index + 8, :] = value
    first, second = hs[0:192, :], hs[192:384, :]
    ys2[0:192, :] = jnp.where(low_half(first), first, roll64(second))
    for slot, n in enumerate((0, 2, 3)):
        ds[72 * slot : 72 * slot + 72, :] = us[72 * n : 72 * n + 72, :]
        ds[216 + 36 * slot : 216 + 36 * slot + 36, :] = ld[plane_rows(1, n), :]
    ds[324:336, :] = jnp.zeros((12, LANES), F32)
    first, second = ds[0:Y_HALF, :], ds[Y_HALF : 2 * Y_HALF, :]
    ys2[Y_REST : Y_REST + Y_HALF, :] = jnp.where(low_half(first), first, roll64(second))
    ys2[Y_CORNER:Y_ROWS, :] = jnp.zeros((Y_ROWS - Y_CORNER, LANES), F32)
    ys2[Y_CORNER : Y_CORNER + 9, :] = roll64(ld[pl.ds(plane_rows(1, 2).start, 9, stride=4), :])
    y_out[...] = ys2[...].astype(BF16)


def t_pack_kernel(xs, ys, us, t_out, ts):
    for index, value in far_halves(xs, ys, 3):
        ts[8 * index : 8 * index + 8, :] = value
    ts[T_LINK : T_LINK + 216, :] = us[0:216, :]
    ts[T_LINK + 216 : T_ROWS, :] = jnp.zeros((T_ROWS - T_LINK - 216, LANES), F32)
    t_out[...] = ts[...].astype(BF16)


def z_pack_kernel(xs, ys, us, ld, tl_ref, z_out, hs, zs):
    for index, value in far_halves(xs, ys, 2):
        hs[8 * index : 8 * index + 8, :] = value
    zs[0:48, :] = hs[pl.ds(0, 48, stride=8), :]
    zs[48:96, :] = hs[pl.ds(1, 48, stride=8), :]
    for slot, n in enumerate((0, 1, 3)):
        zs[Z_LINK + 18 * slot : Z_LINK + 18 * slot + 18, :] = us[pl.ds(72 * n, 18, stride=4), :]
        zs[Z_L + 9 * slot : Z_L + 9 * slot + 9, :] = ld[pl.ds(plane_rows(2, n).start, 9, stride=4), :]
    zs[Z_L + 27 : Z_ROWS, :] = jnp.zeros((Z_ROWS - Z_L - 27, LANES), F32)
    zs[Z_CORNER : Z_CORNER + 9, :] = tl_ref[L_CORNER:L_ROWS, :].astype(F32)[0:9, :]
    z_out[...] = zs[...].astype(BF16)


def full(ref, base):
    def get(ri, c, d):
        return ref[pl.ds(base + 8 * (ri * 9 + c * 3 + d), 8), :]

    return get


def herm(ref, base):
    def get(ri, c, d):
        if c == d:
            return None if ri else ref[pl.ds(base + 8 * c, 8), :]
        low, high = min(c, d), max(c, d)
        value = ref[pl.ds(base + 8 * (3 + 2 * OFF.index((low, high)) + ri), 8), :]
        return -value if ri and c > d else value

    return get


def dagger(get):
    def other(ri, c, d):
        value = get(ri, d, c)
        return -value if ri and value is not None else value

    return other


def dot(left, right, ri, c, d):
    total = None
    for e in range(3):
        for part in range(2):
            a, b = left(part, c, e), right(ri ^ part, e, d)
            if a is None or b is None:
                continue
            term = a * b
            if ri == 0 and part == 1:
                total = -term if total is None else total - term
            else:
                total = term if total is None else total + term
    return total


def held(get):
    table = {(ri, c, d): get(ri, c, d) for ri in range(2) for c in range(3) for d in range(3)}
    return lambda ri, c, d: table[ri, c, d]


def product(left, right, extra=None):
    table = {}
    for c in range(3):
        for d in range(3):
            for ri in range(2):
                value = dot(left, right, ri, c, d)
                if extra is not None:
                    value = value + extra(ri, c, d)
                table[ri, c, d] = value
    return lambda ri, c, d: table[ri, c, d]


def keep(ref, base, get):
    for ri in range(2):
        for c in range(3):
            for d in range(3):
                ref[pl.ds(base + 8 * (ri * 9 + c * 3 + d), 8), :] = get(ri, c, d)
    return full(ref, base)


def anti(left, right):
    entries = [dot(left, right, 1, c, c) for c in range(3)]
    for c, d in OFF:
        entries.append(dot(left, right, 0, c, d) - dot(left, right, 0, d, c))
        entries.append(dot(left, right, 1, c, d) + dot(left, right, 1, d, c))
    return entries


def stage_near(xs, ys, weights, near, base, m):
    for p in range(2):
        for term, (ref, sign) in enumerate(((ys, -1.0), (xs, 1.0))):
            for ri in range(2):
                for spin in range(2):
                    for col in range(3):
                        index = p * 24 + term * 12 + ri * 6 + spin * 3 + col
                        row = base + 8 * index
                        near[row : row + 8, :] = half_component(ref, p, ri, spin, col, m, sign) * weights[8 * p : 8 * p + 8, :]


def hop_sums(far, near, far_base, near_base, hop, hop_base):
    sums = {}
    for p in range(2):
        for term in range(2):
            for spin in range(2):

                def part(ref, base, ri, col):
                    return ref[pl.ds(base + 8 * (p * 24 + term * 12 + ri * 6 + spin * 3 + col), 8), :]

                a = [[part(far, far_base, ri, c) for ri in range(2)] for c in range(3)]
                b = [[part(near, near_base, ri, c) for ri in range(2)] for c in range(3)]
                for c in range(3):
                    for d in range(3):
                        re = a[c][0] * b[d][0] + a[c][1] * b[d][1]
                        im = a[c][1] * b[d][0] - a[c][0] * b[d][1]
                        if (c, d) in sums:
                            sums[c, d] = (sums[c, d][0] + re, sums[c, d][1] + im)
                        else:
                            sums[c, d] = (re, im)
    for c in range(3):
        for d in range(3):
            for ri in range(2):
                hop[pl.ds(hop_base + 8 * (ri * 9 + c * 3 + d), 8), :] = sums[c, d][ri]


class Neighbours:
    def __init__(self, geo, us, ld, tf=None, tl=None, yf=None, zf=None):
        self.geo, self.us, self.ld, self.tf, self.tl, self.yf, self.zf = geo, us, ld, tf, tl, yf, zf

    def link(self, n):
        return self.us[72 * n : 72 * n + 72, :]

    def came_y(self, row, count):
        pieces = []
        if row < Y_HALF:
            stop = min(row + count, Y_HALF)
            pieces.append(roll64(self.yf[Y_REST + row : Y_REST + stop, :]))
            count, row = count - (stop - row), stop
        if count:
            pieces.append(self.yf[Y_REST + row - Y_HALF : Y_REST + row - Y_HALF + count, :])
        return pieces[0] if len(pieces) == 1 else jnp.concatenate(pieces, axis=0)

    def y_next(self, here, came):
        return jnp.where(low_half(here), roll64(here), came)

    def put(self, base, h, value):
        self.geo[pl.ds(base + h, value.shape[0], stride=2), :] = value

    def put_z(self, base, h, value, face):
        self.geo[pl.ds(base + h - 2, value.shape[0], stride=2), :] = value
        self.geo[pl.ds(base + h + 6, face.shape[0], stride=8), :] = face

    def link_next(self, base, h, n, m):
        slot = [k for k in range(4) if k != m].index(n)
        if m == 0:
            self.put(base, h, x_next(self.link(n)))
        elif m == 1:
            self.put(base, h, self.y_next(self.link(n), self.came_y(72 * slot, 72)))
        elif m == 2:
            self.put_z(base, h, self.link(n), self.zf[Z_LINK + 18 * slot : Z_LINK + 18 * slot + 18, :])
        else:
            self.put(base, h, self.tf[72 * slot : 72 * slot + 72, :])

    def here(self, m, n):
        return self.ld[plane_rows(m, n), :]

    def from_t(self, n):
        row = (L_XT, 0, L_ZT)[n]
        return self.tl[row : row + 36, :]

    def from_y(self, n):
        slot = (0, 2, 3).index(n)
        return self.y_next(self.here(1, n), self.came_y(216 + 36 * slot, 36))

    def z_face(self, n):
        slot = (0, 1, 3).index(n)
        return self.zf[Z_L + 9 * slot : Z_L + 9 * slot + 9, :]

    def insertion_next(self, base, h, n, m):
        if m == 0:
            self.put(base, h, x_next(self.here(m, n)))
        elif m == 1:
            self.put(base, h, self.from_y(n))
        elif m == 2:
            self.put_z(base, h, self.here(m, n), self.z_face(n))
        else:
            self.put(base, h, self.from_t(n))

    def corner(self, base, h, m, n):
        if m == 0 and n == 1:
            self.put(base, h, x_next(self.from_y(0)))
        elif m == 0 and n == 2:
            self.put_z(base, h, x_next(self.here(0, 2)), x_next(self.z_face(0)))
        elif m == 0:
            self.put(base, h, x_next(self.from_t(0)))
        elif m == 1 and n == 2:
            face = self.z_face(1)
            came = self.zf[Z_ROWS : Z_ROWS + 9, :]
            self.put_z(base, h, self.from_y(2), jnp.where(low_half(face), roll64(face), came))
        elif m == 1:
            self.put(base, h, self.y_next(self.from_t(1), roll64(self.yf[Y_ROWS : Y_ROWS + 36, :])))
        else:
            self.put_z(base, h, self.from_t(2), self.zf[Z_CORNER : Z_CORNER + 9, :])

    def stage(self, base, pair):
        for h in range(2):
            m, n = pair[h]
            self.put(base + G_UM, h, self.link(m))
            self.put(base + G_UN, h, self.link(n))
            self.link_next(base + G_UN1, h, n, m)
            self.link_next(base + G_UM1, h, m, n)
            self.insertion_next(base + G_LM, h, n, m)
            self.insertion_next(base + G_LN, h, m, n)
            self.corner(base + G_LMN, h, m, n)
            self.put(base + G_L0, h, self.here(m, n))


def plane_force(geo, g, work, acc, a):
    um, un = full(geo, g + G_UM), full(geo, g + G_UN)
    un1, um1 = full(geo, g + G_UN1), full(geo, g + G_UM1)
    lm, ln, lmn, l0 = (herm(geo, g + k) for k in (G_LM, G_LN, G_LMN, G_L0))
    loop = keep(work, 0, product(un1, dagger(um1)))
    inner = keep(work, 144, product(un1, lmn))
    first = product(lm, loop)
    inner = keep(work, 288, product(inner, dagger(um1), first))
    inner = keep(work, 144, product(loop, ln, inner))
    inner = keep(work, 288, product(um, inner))
    loop = keep(work, 144, product(um, loop))
    whole = keep(work, 0, product(loop, dagger(un)))
    common = anti(inner, dagger(un))
    to_m = anti(whole, l0)
    to_n = anti(l0, whole)
    for e in range(9):
        scale = 0.5 if e < 3 else 0.25
        acc[pl.ds(a + 8 * e, 8), :] = scale * (common[e] + to_m[e])
        acc[pl.ds(a + 72 + 8 * e, 8), :] = scale * (common[e] + to_n[e])


def xy_kernel(xs, ys, weights, y_ref, hop, yf, far, near):
    yf[...] = y_ref[0:Y_REST, :].astype(F32)
    for index, value in far_halves(xs, ys, 0):
        far[8 * index : 8 * index + 8, :] = x_next(value)
    stage_near(xs, ys, weights, near, 0, 0)
    low = lane_index() < CX
    for index, value in far_halves(xs, ys, 1):
        row = 384 + 8 * index
        came = yf[8 * (index % 24) : 8 * (index % 24) + 8, :]
        if index < 24:
            far[row : row + 8, :] = roll64(jnp.where(low, came, value))
        else:
            far[row : row + 8, :] = jnp.where(low, roll64(value), came)
    stage_near(xs, ys, weights, near, 384, 1)

    def one_hop(m, carry):
        base = pl.multiple_of(m * 384, 8)
        hop_sums(far, near, base, base, hop, pl.multiple_of(m * 144, 8))
        return carry

    lax.fori_loop(0, 2, one_hop, 0)


def t_kernel(xs, ys, us, ld, weights, tl_ref, t_ref, y_ref, hop, acc, near_z, tl, tf, yf, near, geo, work):
    tl[...] = tl_ref[...].astype(F32)
    tf[...] = t_ref[T_LINK:T_ROWS, :].astype(F32)
    yf[...] = y_ref[...].astype(F32)
    geo[920:1304, :] = t_ref[0:384, :].astype(F32)
    stage_near(xs, ys, weights, near, 0, 3)
    stage_near(xs, ys, weights, near_z, 0, 2)
    hop_sums(geo, near, 920, 0, hop, 0)
    Neighbours(geo, us, ld, tf, tl, yf).stage(0, T_PAIR)
    plane_force(geo, 0, work, acc, 0)


def last_kernel(
    xs, ys, us, ld, tl_ref, t_ref, y_ref, z_ref, hop_xy, hop_t, acc_t, near, out,
    tl, tf, yf, zf, far, hop, geo, work, acc,
):
    tl[...] = tl_ref[...].astype(F32)
    tf[...] = t_ref[T_LINK:T_ROWS, :].astype(F32)
    yf[...] = y_ref[...].astype(F32)
    zf[...] = z_ref[0 : Z_ROWS + 16, :].astype(F32)
    for index, value in far_halves(xs, ys, 2):
        far[8 + 8 * index - 2 : 8 + 8 * index + 6, :] = value
    far[pl.ds(8 + 6, 48, stride=8), :] = zf[0:48, :]
    far[pl.ds(8 + 7, 48, stride=8), :] = zf[48:96, :]
    hop_sums(far, near, 8, 0, hop, 0)
    places = Neighbours(geo, us, ld, tf, tl, yf, zf)
    for pair in range(2):
        places.stage(G_ROWS * pair, Z_PAIRS[pair])

    def one_pair(pair, carry):
        plane_force(geo, pl.multiple_of(pair * G_ROWS, 8), work, acc, pl.multiple_of(pair * 144, 8))
        return carry

    lax.fori_loop(0, 2, one_pair, 0)
    acc[288:432, :] = acc_t[...]

    even = lax.broadcasted_iota(jnp.int32, (8, LANES), 0) % 2 == 0
    places.put(0, 0, places.link(0))
    places.put(0, 1, places.link(1))
    places.put(144, 0, places.link(2))
    places.put(144, 1, places.link(3))
    halves = [((hop_xy, 0), (hop_xy, 144)), ((hop, 0), (hop_t, 0))]
    for pair in range(2):
        table = {}
        for ri in range(2):
            for c in range(3):
                for d in range(3):
                    row = 8 * (ri * 9 + c * 3 + d)
                    a, b = (ref[base + row : base + row + 8, :] for ref, base in halves[pair])
                    table[ri, c, d] = jnp.where(even, a + pltpu.roll(a, 7, 0), b + pltpu.roll(b, 1, 0))
        entries = anti(full(geo, 144 * pair), lambda ri, c, d: table[ri, c, d])
        for e in range(9):
            row = 432 + 72 * pair + 8 * e
            acc[row : row + 8, :] = entries[e] if e < 3 else 0.5 * entries[e]

    sources = [
        [(0, 0), (2, 0), (4, 0), (6, 0)],
        [(0, 1), (3, 0), (4, 1), (6, 1)],
        [(1, 0), (1, 1), (2, 1), (7, 0)],
        [(3, 1), (5, 0), (5, 1), (7, 1)],
    ]
    zero = jnp.zeros((4, LANES), F32)
    for m in range(4):
        values = []
        for e in range(9):
            total = None
            for slot, h in sources[m]:
                piece = acc[pl.ds(72 * slot + 8 * e + h, 4, stride=2), :]
                total = piece if total is None else total + piece
            values.append(total)
        trace = (values[0] + values[1] + values[2]) * (1.0 / 3.0)
        for c in range(3):
            for d in range(3):
                if c == d:
                    re, im = zero, values[c] - trace
                else:
                    e = 3 + 2 * OFF.index((min(c, d), max(c, d)))
                    re, im = (values[e] if c < d else -values[e]), values[e + 1]
                row = 72 * m + 4 * (3 * c + d)
                out[row : row + 4, :] = re
                out[row + 36 : row + 40, :] = im


def vmem(rows):
    return pltpu.VMEM((rows, LANES), F32)


IN_VMEM = pl.BlockSpec(memory_space=pltpu.VMEM)


def call(kernel, name, in_specs, outs, scratch, flops, out_specs=IN_VMEM):
    shapes = [jax.ShapeDtypeStruct((rows, LANES), kind) for rows, kind in outs]
    return pl.pallas_call(
        kernel,
        out_shape=shapes,
        in_specs=in_specs,
        out_specs=[out_specs] * len(shapes),
        scratch_shapes=[vmem(k) if isinstance(k, int) else k for k in scratch],
        compiler_params=pltpu.CompilerParams(vmem_limit_bytes=24 * 1024 * 1024),
        cost_estimate=pl.CostEstimate(flops=flops, bytes_accessed=1000000, transcendentals=0),
        name=name,
    )


def passed_back(block, *axes):
    sizes = [lax.axis_size(axis) for axis in axes]
    route = []
    for place in np.ndindex(*sizes):
        source = [(k + 1) % size for k, size in zip(place, sizes)]
        route.append((int(np.ravel_multi_index(source, sizes)), int(np.ravel_multi_index(place, sizes))))
    return lax.ppermute(block, axes if len(axes) > 1 else axes[0], route)


def shards(solution_x, solution_y, links, pole_coef):
    inputs = [solution_x.reshape(384, LANES), solution_y.reshape(384, LANES), links.reshape(288, LANES), pole_coef]
    xs, ys, us, local, weights, to_tl = call(
        first_kernel,
        "insertions",
        [pl.BlockSpec(memory_space=pltpu.HBM)] * 4,
        [(384, F32), (384, F32), (U_ROWS, F32), (LD_ROWS, F32), (16, F32), (L_ROWS, BF16)],
        [pltpu.VMEM((384, LANES), BF16)] * 2
        + [pltpu.VMEM((288, LANES), BF16), pltpu.SMEM((4,), F32), 432, L_ROWS, pltpu.SemaphoreType.DMA((4,))],
        1000000,
    )(*[pltpu.with_memory_space_constraint(array, pltpu.HBM) for array in inputs])
    tl_came = passed_back(to_tl, "ta")
    (to_t,) = call(t_pack_kernel, "pack_t", [IN_VMEM] * 3, [(T_ROWS, BF16)], [T_ROWS], 500000)(xs, ys, us)
    t_came = passed_back(to_t, "ta")
    (to_y,) = call(y_pack_kernel, "pack_y", [IN_VMEM] * 4, [(Y_ROWS, BF16)], [384, 336, Y_ROWS], 500000)(xs, ys, us, local)
    y_came = passed_back(jnp.concatenate([to_y, tl_came[0:48]]), "gy")
    (to_z,) = call(z_pack_kernel, "pack_z", [IN_VMEM] * 5, [(Z_ROWS, BF16)], [384, Z_ROWS], 500000)(
        xs, ys, us, local, tl_came
    )
    z_block = jnp.concatenate(
        [to_z, y_came[Y_CORNER : Y_CORNER + 16], t_came[T_ROWS - 16 :]]
    )
    z_came = passed_back(z_block, "gz")
    (hop_xy,) = call(
        xy_kernel, "hop_xy", [IN_VMEM] * 4, [(288, F32)], [Y_REST, 768, 768], 2000000
    )(xs, ys, weights, y_came)
    hop_t, acc_t, near_z = call(
        t_kernel,
        "force_t",
        [IN_VMEM] * 8,
        [(144, F32), (144, F32), (384, F32)],
        [L_ROWS, T_ROWS - T_LINK, Y_ROWS + 48, 384, 1304, 432],
        2000000,
    )(xs, ys, us, local, weights, tl_came, t_came, y_came)
    (force,) = call(
        last_kernel,
        "force",
        [IN_VMEM] * 12,
        [(288, F32)],
        [L_ROWS, T_ROWS - T_LINK, Y_ROWS + 48, Z_ROWS + 16, 400, 144, 2 * G_ROWS, 432, 592],
        4000000,
        out_specs=pl.BlockSpec(),
    )(xs, ys, us, local, tl_came, t_came, y_came, z_came, hop_xy, hop_t, acc_t, near_z)
    return force.reshape(links.shape)


def solution(mesh):
    placed = P(None, None, "ta", "gz", "gy")
    return jax.shard_map(
        shards, mesh=mesh, in_specs=(placed, placed, placed, P()), out_specs=placed, check_vma=False
    )
```
